128 devices in a mesh: row: 16 (over z_hi, y, core), col: 8 (over x, z_lo).
Axes of the slice: x: 4, y: 4, z: 4 (z_hi: 2, z_lo: 2; z = z_hi * 2 + z_lo), core: 2. Of those that a mesh axis runs over, the one named last changes fastest.
Arguments:
- vectors_in: float32 [16384, 16384], P('row', 'col'), may hold values from -6 to 6
- reflectors: float32 [8, 128, 128], P(None, 'row', 'col'), may hold values from -6 to 6
- offsets: int32 [8], replicated, may hold values from 1 to 64, as said below
Outputs:
- vectors_out: float32 [16384, 16384], P('row', 'col')
The draws below stay inside these ranges and needn't reach their ends.
Inputs may be any that keep to these rules, and one draw needn't show every extreme that they name: `offsets`: each sweep's first window begins within the first half of a reflector's length; the values 1 and 64 both occur in every draw.
All inputs are finite; a program needn't handle non-finite values.
Results may differ from the reference program's by a relative error of at most 0.0002.
Values sent between devices are 32-bit elements; how exact they have to be, the bound alone decides.
A program may use at most 128 MiB of HBM per device.

```python
import jax
import jax.numpy as jnp
from jax import lax

B = 128
M = 16384
SWEEPS = 8
ROWS = 16384
WINDOWS = 128


def draw_offsets(key, part):
    key = jax.random.fold_in(key, 7)
    first, second = jax.random.split(key)
    values = jax.random.randint(first, (SWEEPS,), 1, B // 2 + 1, dtype=jnp.int32)
    order = jax.random.permutation(second, SWEEPS)
    values = values.at[order[0]].set(B // 2)
    values = values.at[order[1]].set(1)
    return values


def block_levels(key, shape, cuts, smallest, top_value):
    gain = 1.0
    for position, shards_of in cuts:
        heights = jax.random.uniform(jax.random.fold_in(jax.random.fold_in(key, 6), position), (shards_of,), jnp.float32, smallest / len(cuts), top_value / len(cuts))
        gain = gain * jnp.repeat(jnp.exp(heights), shape[position] // shards_of).reshape((-1,) + (1,) * (len(shape) - 1 - position))
    return gain


def noise(stream_key, dims, spread, limit, cuts=(), kind=jnp.bfloat16):
    array = jax.random.normal(stream_key, dims, jnp.float32) * spread
    if len(cuts) > 0:
        array = block_levels(stream_key, dims, cuts, -0.22, 0.18) * array
    return jnp.clip(array, min=-limit, max=limit).astype(kind)


def setup_inputs(seed: int = 0) -> dict:
    streams_of = jax.random.split(jax.random.key(seed), 4)
    return {
        "vectors_in": noise(streams_of[0], (ROWS, M), 1.0, 6.0, ((0, 16), (1, 8)), jnp.float32),
        "reflectors": noise(streams_of[1], (SWEEPS, WINDOWS, B), 1.0, 6.0, ((1, 16), (2, 8)), jnp.float32),
        "offsets": draw_offsets(jax.random.fold_in(streams_of[3], 71), 0),
    }


def reflect(block, vecs, first_row, total_rows):
    count = vecs.shape[0]
    width = vecs.shape[1]
    index = first_row + jnp.arange(count * width, dtype=jnp.int32).reshape(count, width)
    vecs = jnp.where((index >= 0) & (index < total_rows), vecs, jnp.float32(0.0))
    scale = 2.0 / (jnp.sum(vecs * vecs, axis=1) + 1e-6)
    tiles = block.reshape(count, width, -1)
    coeff = jnp.einsum("kb,kbc->kc", vecs, tiles, precision=lax.Precision.HIGHEST) * scale[:, None]
    return (tiles - vecs[:, :, None] * coeff[:, None, :]).reshape(count * width, -1)


def reference(vectors_in, reflectors, offsets):
    total = vectors_in.shape[0]
    padded = jnp.concatenate([vectors_in, jnp.zeros((B, vectors_in.shape[1]), vectors_in.dtype)], axis=0)
    for sweep in range(SWEEPS):
        start = offsets[sweep].astype(jnp.int32)
        window = lax.dynamic_slice_in_dim(padded, start, total, 0)
        window = reflect(window, reflectors[sweep], start, total)
        padded = lax.dynamic_update_slice_in_dim(padded, window, start, 0)
    return padded[:total]
```

```python
import functools

import jax
import jax.numpy as jnp
from jax import lax
from jax.experimental import pallas as pl
from jax.experimental.pallas import tpu as pltpu
from jax.sharding import PartitionSpec as P

MESH = pl.DeviceIdType.MESH
F32 = jnp.float32
BF16 = jnp.bfloat16
EPS = 1e-6
S = 8
W = 8
B = 128
N = 80
LAST = 64
MIB = 1 << 20


def exact_dot(a, b, dims):
    return lax.dot_general(
        a, b, (dims, ((), ())), precision=lax.Precision.HIGHEST, preferred_element_type=F32
    )


def split(x):
    hi = x.astype(BF16)
    return hi, (x - hi.astype(F32)).astype(BF16)


def iota(shape, axis):
    return lax.broadcasted_iota(jnp.int32, shape, axis)


def unit_inverse(n, row_s, col_s, eye):
    low = ((row_s // 2) == (col_s // 2)) & (row_s > col_s)
    inv = eye - jnp.where(low, n, 0.0)
    for b in (2, 4):
        low = ((row_s // (2 * b)) == (col_s // (2 * b))) & ((row_s // b) > (col_s // b))
        part = exact_dot(jnp.where(low, n, 0.0), inv, ((1,), (0,)))
        inv = inv - exact_dot(inv, part, ((1,), (0,)))
    return inv


def first_kernel(
    R, C, CHUNKS,
    off_ref, e_hbm, refl_hbm,
    e_ref, y_ref, c_ref,
    refl, mine, gat, hi_ref, lo_ref, vt, wt, p_ref, msg, near, recv,
    refl_sem, e_sem, out_sem, gat_sem, msg_sem, near_sem, p_sem, recv_sem,
):
    r = lax.axis_index("row")
    c = lax.axis_index("col")
    up = lax.rem(r + R - 1, R)
    down = lax.rem(r + 1, R)
    rows, cols = e_ref.shape
    step = rows // W
    width = cols // CHUNKS

    refl_copy = pltpu.make_async_copy(refl_hbm, refl, refl_sem)
    refl_copy.start()
    loads = []
    for i in range(W):
        part = pl.ds(i * step, step)
        load = pltpu.make_async_copy(e_hbm.at[part], e_ref.at[part], e_sem.at[i])
        load.start()
        loads.append(load)

    barrier = pltpu.get_barrier_semaphore()
    for d in range(1, C):
        pl.semaphore_signal(barrier, inc=1, device_id=(r, lax.rem(c + d, C)), device_id_type=MESH)
    for d in range(C):
        pl.semaphore_signal(barrier, inc=1, device_id=(up, lax.rem(c + d, C)), device_id_type=MESH)
    pl.semaphore_signal(barrier, inc=1, device_id=(down, c), device_id_type=MESH)

    refl_copy.wait()
    piece = refl.shape[2]
    tile = jnp.concatenate([refl[:, k, :] for k in range(W)], axis=1)
    mine[...] = tile
    gat[0, c] = tile
    pl.semaphore_wait(barrier, 2 * C)

    sends = []
    for d in range(1, C):
        sends.append(pltpu.make_async_remote_copy(
            src_ref=mine, dst_ref=gat.at[0, c], send_sem=out_sem.at[0, d], recv_sem=gat_sem.at[0, c],
            device_id=(r, lax.rem(c + d, C)), device_id_type=MESH))
    for d in range(C):
        sends.append(pltpu.make_async_remote_copy(
            src_ref=mine, dst_ref=gat.at[1, c], send_sem=out_sem.at[1, d], recv_sem=gat_sem.at[1, c],
            device_id=(down, lax.rem(c + d, C)), device_id_type=MESH))
    for copy in sends:
        copy.start()

    for i in range(W):
        loads[i].wait()

        @pl.loop(0, cols // 512)
        def _(j):
            at = (pl.ds(i * step, step), pl.ds(pl.multiple_of(j * 512, 512), 512))
            hi, lo = split(e_ref[at])
            hi_ref[at] = hi
            lo_ref[at] = lo

    for d in range(1, C):
        src = lax.rem(c + d, C)
        pltpu.make_async_remote_copy(
            src_ref=mine, dst_ref=gat.at[0, src], send_sem=out_sem.at[0, d], recv_sem=gat_sem.at[0, src],
            device_id=(r, src), device_id_type=MESH).wait_recv()
    for src in range(C):
        pltpu.make_async_remote_copy(
            src_ref=mine, dst_ref=gat.at[1, src], send_sem=out_sem.at[1, src], recv_sem=gat_sem.at[1, src],
            device_id=(up, src), device_id_type=MESH).wait_recv()

    lane = iota((S, B), 1)
    parts = [[gat[0, q] for q in range(C)], [gat[1, q] for q in range(C)]]

    def window(kind, k):
        out = jnp.zeros((S, B), F32)
        for q in range(C):
            turn = (q * piece - k * piece) % B
            x = parts[kind][q]
            x = x if turn == 0 else pltpu.roll(x, turn, 1)
            out = jnp.where((lane >= q * piece) & (lane < (q + 1) * piece), x, out)
        return out

    sub = iota((S, B), 0)
    off = jnp.zeros((S, B), jnp.int32)
    for s in range(S):
        off = jnp.where(sub == s, off_ref[s], off)

    vt[...] = jnp.zeros_like(vt)
    wt[...] = jnp.zeros_like(wt)
    tau_x = [None, None]
    for g in range(W + 1):
        x = window(1, W - 1) if g == 0 else window(0, g - 1)
        for b in range(7):
            x = jnp.where((off >> b) & 1 == 1, pltpu.roll(x, 1 << b, 1), x)
        here = jnp.where(lane >= off, x, 0.0)
        over = jnp.where(lane < off, x, 0.0)
        if g == 0:
            here = jnp.where(r > 0, here, 0.0)
            over = jnp.where(r > 0, over, 0.0)
        if g == W:
            over = jnp.where(r < R - 1, over, 0.0)
        square = here * here + over * over
        tau = 2.0 / (jnp.sum(square, axis=1, keepdims=True) + EPS)
        if g == 0:
            tau_x[0] = jnp.where(r > 0, tau, 0.0)
        if g == W:
            tau_x[1] = tau
        weight = 1.0 if g in (0, W) else tau
        rows_g = pl.ds(g * S, S)
        if g > 0:
            vt[rows_g, pl.ds((g - 1) * B, B)] = here
            wt[rows_g, pl.ds((g - 1) * B, B)] = here * weight
        if g < W:
            vt[rows_g, pl.ds(g * B, B)] = over
            wt[rows_g, pl.ds(g * B, B)] = over * weight

    ri, ci = iota((N, N), 0), iota((N, N), 1)
    row_s, col_s = ri % S, ci % S
    row_g, col_g = ri // S, ci // S
    eye = jnp.where(ri == ci, 1.0, 0.0).astype(F32)
    row_x = (row_g == 0) | (row_g == W)
    col_x = (col_g == 0) | (col_g == W)
    gram = exact_dot(vt[...], wt[...], ((1,), (1,)))
    gram = jnp.where(row_s > col_s, gram, 0.0)
    inv = unit_inverse(jnp.where(col_x, 0.0, gram), row_s, col_s, eye)
    f = exact_dot(inv, vt[...], ((1,), (0,)))
    m = exact_dot(inv, jnp.where(col_x, gram, 0.0), ((1,), (0,)))
    pad = jnp.zeros((S, B - N), F32)
    m_top = jnp.concatenate([m[0:S], pad], axis=1)
    m_low = jnp.concatenate([m[LAST:LAST + S], pad], axis=1)
    msg[0] = m_top
    msg[1] = m_low
    for i, there in ((0, up), (1, down)):
        copy = pltpu.make_async_remote_copy(
            src_ref=msg.at[i], dst_ref=near.at[i], send_sem=msg_sem.at[i], recv_sem=near_sem.at[i],
            device_id=(there, c), device_id_type=MESH)
        copy.start()
        sends.append(copy)

    f_hi, f_lo = split(f)
    f_both = jnp.concatenate([f_hi, f_lo], axis=0)
    for j in range(CHUNKS):
        at = pl.ds(j * width, width)
        both = jnp.dot(f_both, hi_ref[:, at], preferred_element_type=F32)
        p = both[:N] + both[N:] + jnp.dot(f_hi, lo_ref[:, at], preferred_element_type=F32)
        p_ref[:, at] = p
        hi, lo = split(p)
        c_ref[0:N, at] = hi
        c_ref[N:2 * N, at] = lo
        c_ref[2 * N:, at] = hi
        for i, there, first in ((0, up, 0), (1, down, LAST)):
            copy = pltpu.make_async_remote_copy(
                src_ref=p_ref.at[pl.ds(first, S), at], dst_ref=recv.at[i, :, at],
                send_sem=p_sem.at[i, j], recv_sem=recv_sem.at[i, j],
                device_id=(there, c), device_id_type=MESH)
            copy.start()
            sends.append(copy)

    for i, there in ((0, down), (1, up)):
        pltpu.make_async_remote_copy(
            src_ref=msg.at[i], dst_ref=near.at[i], send_sem=msg_sem.at[i], recv_sem=near_sem.at[i],
            device_id=(there, c), device_id_type=MESH).wait_recv()
    from_down = pltpu.roll(near[0], LAST, 1)
    from_up = pltpu.roll(near[1], B - LAST, 1)
    a_top = jnp.where(lane < S, m_top + jnp.where(r > 0, from_up, 0.0), 0.0) * tau_x[0]
    a_low = jnp.where((lane >= LAST) & (lane < LAST + S), m_low + jnp.where(r < R - 1, from_down, 0.0), 0.0) * tau_x[1]
    zero = jnp.zeros((S, B), F32)
    a = jnp.concatenate([a_top] + [zero] * (W - 1) + [a_low, zero], axis=0)[:, :N]
    tau_col = jnp.concatenate(
        [jnp.broadcast_to(tau_x[0], (S, N))] + [jnp.zeros((S, N), F32)] * (W - 1)
        + [jnp.broadcast_to(tau_x[1], (S, N)), jnp.zeros((S, N), F32)], axis=0)
    tau_row = jnp.sum(jnp.where(ri == ci, tau_col, 0.0), axis=0, keepdims=True)
    t = unit_inverse(a, row_s, col_s, eye) * tau_row
    inner = jnp.where(row_x, 0.0, m)
    left = jnp.where(row_x & (ri == ci), 1.0, 0.0) - inner
    k_t = jnp.where(col_x, exact_dot(left, t, ((1,), (0,))), eye)
    y = exact_dot(wt[...], k_t, ((0,), (0,)))
    y_hi, y_lo = split(y)
    y_ref[:, 0:N] = y_hi
    y_ref[:, N:2 * N] = y_hi
    y_ref[:, 2 * N:] = y_lo

    for j in range(CHUNKS):
        at = pl.ds(j * width, width)
        for i, there in ((0, down), (1, up)):
            pltpu.make_async_remote_copy(
                src_ref=p_ref.at[pl.ds(0, S), at], dst_ref=recv.at[i, :, at],
                send_sem=p_sem.at[i, j], recv_sem=recv_sem.at[i, j],
                device_id=(there, c), device_id_type=MESH).wait_recv()
        for first, i, keep in ((0, 1, r > 0), (LAST, 0, r < R - 1)):
            got = jnp.where(keep, recv[i, :, at], 0.0)
            x = jnp.concatenate([p_ref[first:first + S, at] + got, p_ref[first + S:first + 2 * S, at]], axis=0)
            hi, lo = split(x)
            c_ref[first:first + 2 * S, at] = hi
            c_ref[N + first:N + first + 2 * S, at] = lo
            c_ref[2 * N + first:2 * N + first + 2 * S, at] = hi
    for copy in sends:
        copy.wait_send()


def second_kernel(parts, e_ref, y_ref, c_ref, o_hbm, buf, sem):
    width = buf.shape[1] // parts

    def store(j):
        at = pl.ds(pl.multiple_of(j * width, width), width)
        return pltpu.make_async_copy(buf.at[:, at], o_hbm.at[:, at], sem.at[j])

    @pl.loop(0, parts)
    def _(j):
        at = pl.ds(pl.multiple_of(j * width, width), width)
        buf[:, at] = e_ref[:, at] - jnp.dot(y_ref[...], c_ref[:, at], preferred_element_type=F32)
        store(j).start()

    @pl.loop(0, parts)
    def _(j):
        store(j).wait()


def solution(mesh):
    R, C = mesh.shape["row"], mesh.shape["col"]

    def body(vectors_in, reflectors, offsets):
        rows, cols = vectors_in.shape
        chunks = 4 if cols % 2048 == 0 else 1
        vmem = pl.BlockSpec(memory_space=pltpu.VMEM)
        anywhere = pl.BlockSpec(memory_space=pl.ANY)
        dma = pltpu.SemaphoreType.DMA
        e, y, coeff = pl.pallas_call(
            functools.partial(first_kernel, R, C, chunks),
            out_shape=(
                pltpu.VMEM((rows, cols), F32),
                pltpu.VMEM((rows, 3 * N), BF16),
                pltpu.VMEM((3 * N, cols), BF16),
            ),
            in_specs=[pl.BlockSpec(memory_space=pltpu.SMEM), anywhere, anywhere],
            out_specs=(vmem, vmem, vmem),
            scratch_shapes=[
                pltpu.VMEM(reflectors.shape, F32),
                pltpu.VMEM((S, B), F32),
                pltpu.VMEM((2, C, S, B), F32),
                pltpu.VMEM((rows, cols), BF16),
                pltpu.VMEM((rows, cols), BF16),
                pltpu.VMEM((N, rows), F32),
                pltpu.VMEM((N, rows), F32),
                pltpu.VMEM((N, cols), F32),
                pltpu.VMEM((2, S, B), F32),
                pltpu.VMEM((2, S, B), F32),
                pltpu.VMEM((2, S, cols), F32),
                dma, dma((W,)), dma((2, C)), dma((2, C)), dma((2,)), dma((2,)), dma((2, chunks)), dma((2, chunks)),
            ],
            compiler_params=pltpu.CompilerParams(
                collective_id=0, has_side_effects=True, vmem_limit_bytes=24 * MIB
            ),
            name="reflect_one",
        )(
            offsets,
            pltpu.with_memory_space_constraint(vectors_in, pltpu.HBM),
            pltpu.with_memory_space_constraint(reflectors, pltpu.HBM),
        )
        parts = max(1, cols // 256)
        return pl.pallas_call(
            functools.partial(second_kernel, parts),
            out_shape=jax.ShapeDtypeStruct((rows, cols), F32),
            in_specs=[vmem, vmem, vmem],
            out_specs=anywhere,
            scratch_shapes=[pltpu.VMEM((rows, cols), F32), dma((parts,))],
            compiler_params=pltpu.CompilerParams(vmem_limit_bytes=16 * MIB),
            name="reflect_two",
        )(*(pltpu.with_memory_space_constraint(x, pltpu.VMEM) for x in (e, y, coeff)))

    in_specs = (P("row", "col"), P(None, "row", "col"), P())
    return jax.shard_map(body, mesh=mesh, in_specs=in_specs, out_specs=P("row", "col"), check_vma=False)
```

```python
import functools

import jax
import jax.numpy as jnp
from jax import lax
from jax.experimental import pallas as pl
from jax.experimental.pallas import tpu as pltpu
from jax.sharding import PartitionSpec as P

MESH = pl.DeviceIdType.MESH
F32 = jnp.float32
BF16 = jnp.bfloat16
EPS = 1e-6
S = 8
W = 8
B = 128
I = S * W
N = I + 2 * S
MIB = 1 << 20


def split(x):
    hi = x.astype(BF16)
    return hi, (x - hi.astype(F32)).astype(BF16)


def wide(x, width):
    return jnp.concatenate([x] * (width // B), axis=1) if width > B else x


def row_of(x, i):
    return jnp.broadcast_to(x[i:i + 1], x.shape)


def gather_rows(tiles, i):
    sub = lax.broadcasted_iota(jnp.int32, tiles[0].shape, 0)
    out = jnp.zeros_like(tiles[0])
    for s, tile in enumerate(tiles):
        out = jnp.where(sub == s, row_of(tile, i), out)
    return out


def lane_sum(x):
    return jnp.broadcast_to(jnp.sum(x, axis=1, keepdims=True), x.shape)


def solve(u, own, after, before, tau, width):
    p, c, nexts, prevs = [], [], [], []
    for s in range(S):
        acc = u[s]
        for t in range(s):
            acc = acc - wide(own(s, t), width) * c[t]
            acc = acc - wide(after(s, t), width) * nexts[t]
            acc = acc - wide(before(s, t), width) * prevs[t]
        p.append(acc)
        c.append(acc * wide(tau(s), width))
        nexts.append(pltpu.roll(c[s], W - 1, 0))
        prevs.append(pltpu.roll(c[s], 1, 0))
    return p, c


def first_kernel(
    R, C, CHUNKS,
    off_hbm, e_hbm, refl_hbm,
    e_ref, y_ref, c_ref,
    off_ref, refl, mine, gat, hi_ref, lo_ref, vt, coef, fact, edge, top, low_ref, top_ref, msg, near, recv,
    off_sem, refl_sem, e_sem, out_sem, gat_sem, edge_sem, top_sem, msg_sem, near_sem, p_sem, recv_sem,
):
    r = lax.axis_index("row")
    c = lax.axis_index("col")
    up = lax.max(r - 1, 0)
    down = lax.min(r + 1, R - 1)
    has_up, has_down = r > 0, r < R - 1
    rows, cols = e_ref.shape
    step = rows // W
    width = cols // CHUNKS
    piece = refl.shape[2]

    barrier = pltpu.get_barrier_semaphore()
    for d in range(1, C):
        pl.semaphore_signal(barrier, inc=1, device_id=(r, lax.rem(c + d, C)), device_id_type=MESH)

    @pl.when(has_up)
    def _():
        pl.semaphore_signal(barrier, inc=1, device_id=(up, c), device_id_type=MESH)

    @pl.when(has_down)
    def _():
        pl.semaphore_signal(barrier, inc=1, device_id=(down, c), device_id_type=MESH)

    refl_copy = pltpu.make_async_copy(refl_hbm, refl, refl_sem)
    refl_copy.start()
    off_copy = pltpu.make_async_copy(off_hbm, off_ref, off_sem)
    off_copy.start()
    loads = []
    for i in range(W):
        part = pl.ds(i * step, step)
        load = pltpu.make_async_copy(e_hbm.at[part], e_ref.at[part], e_sem.at[i])
        load.start()
        loads.append(load)

    refl_copy.wait()
    tile = jnp.concatenate([refl[s] for s in range(S)], axis=1)
    mine[...] = tile
    pl.semaphore_wait(barrier, C - 1 + lax.min(r, 1) + lax.min(R - 1 - r, 1))

    sends = []
    for d in range(1, C):
        sends.append(pltpu.make_async_remote_copy(
            src_ref=mine, dst_ref=gat.at[c], send_sem=out_sem.at[d], recv_sem=gat_sem.at[c],
            device_id=(r, lax.rem(c + d, C)), device_id_type=MESH))
    for copy in sends:
        copy.start()
    gat[c] = tile

    def edge_copy(to):
        return pltpu.make_async_remote_copy(
            src_ref=edge, dst_ref=top, send_sem=edge_sem, recv_sem=top_sem,
            device_id=(to, c), device_id_type=MESH)

    def msg_copy(i, to):
        return pltpu.make_async_remote_copy(
            src_ref=msg.at[i], dst_ref=near.at[i], send_sem=msg_sem.at[i], recv_sem=near_sem.at[i],
            device_id=(to, c), device_id_type=MESH)

    def sum_copy(i, j, to):
        at = pl.ds(j * width, width)
        return pltpu.make_async_remote_copy(
            src_ref=(top_ref, low_ref)[i].at[:, at], dst_ref=recv.at[i, :, at],
            send_sem=p_sem.at[i, j], recv_sem=recv_sem.at[i, j],
            device_id=(to, c), device_id_type=MESH)

    @pl.when(r == 0)
    def _():
        top[...] = jnp.zeros_like(top)
        near[1] = jnp.zeros((S, B), F32)
        recv[1] = jnp.zeros((S, cols), F32)

    @pl.when(r == R - 1)
    def _():
        near[0] = jnp.zeros((S, B), F32)
        recv[0] = jnp.zeros((S, cols), F32)

    vt[...] = jnp.zeros_like(vt)

    for i in range(W):
        loads[i].wait()

        @pl.loop(0, cols // 512)
        def _(j):
            at = (pl.ds(i * step, step), pl.ds(pl.multiple_of(j * 512, 512), 512))
            hi, lo = split(e_ref[at])
            hi_ref[at] = hi
            lo_ref[at] = lo

    off_copy.wait()
    lane = lax.broadcasted_iota(jnp.int32, (S, B), 1)
    sub = lax.broadcasted_iota(jnp.int32, (S, B), 0)

    for d in range(1, C):
        src = lax.rem(c + d, C)
        pltpu.make_async_remote_copy(
            src_ref=mine, dst_ref=gat.at[src], send_sem=out_sem.at[d], recv_sem=gat_sem.at[src],
            device_id=(r, src), device_id_type=MESH).wait_recv()

    parts = [gat[q] for q in range(C)]
    turned, heres, overs, taus = [], [], [], []
    for s in range(S):
        x = jnp.zeros((W, B), F32)
        for q in range(C):
            turn = ((q - s) * piece) % B
            y = parts[q] if turn == 0 else pltpu.roll(parts[q], turn, 1)
            x = jnp.where((lane >= q * piece) & (lane < (q + 1) * piece), y, x)
        o = off_ref[s]
        for b in range(7):
            x = jnp.where(((o >> b) & 1) == 1, pltpu.roll(x, 1 << b, 1), x)
        turned.append(x)
    edge[...] = gather_rows(turned, W - 1)

    @pl.when(has_down)
    def _():
        edge_copy(down).start()

    for s in range(S):
        x, o = turned[s], off_ref[s]
        here = jnp.where(lane >= o, x, 0.0)
        over = jnp.where(lane < o, x, 0.0)
        whole = here * here + jnp.where((sub < W - 1) | has_down, over * over, 0.0)
        taus.append(2.0 / (lane_sum(whole) + EPS))
        over = jnp.where(sub < W - 1, over, 0.0)
        heres.append(here)
        overs.append(over)
        fact[s] = jnp.where(sub < W - 1, taus[s], 0.0)
    tau_low = gather_rows(taus, W - 1)
    for q in range(S // 2):
        for t in range(W):
            pair = []
            for s in (2 * q, 2 * q + 1):
                x = jnp.where(sub == t, heres[s], 0.0)
                if t > 0:
                    x = x + jnp.where(sub == t - 1, overs[s], 0.0)
                pair.append(x)
            hi, lo = split(jnp.concatenate(pair, axis=0))
            at = pl.ds(t * B, B)
            vt[q * 2 * W:(q + 1) * 2 * W, at] = hi
            vt[N + q * 2 * W:N + (q + 1) * 2 * W, at] = lo
            vt[2 * N + q * 2 * W:2 * N + (q + 1) * 2 * W, at] = hi

    def pair_index(s, t):
        return s * (s - 1) // 2 + t

    for s in range(S):
        for t in range(s):
            own = lane_sum(heres[s] * heres[t] + overs[s] * overs[t])
            after = lane_sum(overs[s] * pltpu.roll(heres[t], W - 1, 0))
            before = lane_sum(heres[s] * pltpu.roll(overs[t], 1, 0))
            n = pair_index(s, t)
            coef[0, n] = own
            coef[1, n] = after
            coef[2, n] = before

    def solved(u, w):
        return solve(
            u, lambda s, t: coef[0, pair_index(s, t)], lambda s, t: coef[1, pair_index(s, t)],
            lambda s, t: coef[2, pair_index(s, t)], lambda s: fact[s], w)

    first_rows = []
    for j in range(CHUNKS):
        at = pl.ds(j * width, width)
        both = jnp.dot(vt[0:2 * N, :], hi_ref[:, at], preferred_element_type=F32)
        u = both[:I] + both[N:N + I] + jnp.dot(vt[0:I, :], lo_ref[:, at], preferred_element_type=F32)
        p, cs = solved([u[s * W:(s + 1) * W] for s in range(S)], width)
        low_ref[:, at] = gather_rows(p, W - 1)

        @pl.when(has_down)
        def _():
            sum_copy(1, j, down).start()

        first_rows.append([x[0:1] for x in cs])
        for q in range(S // 2):
            hi, lo = split(jnp.concatenate(cs[2 * q:2 * q + 2], axis=0))
            c_ref[q * 2 * W:(q + 1) * 2 * W, at] = hi
            c_ref[N + q * 2 * W:N + (q + 1) * 2 * W, at] = lo
            c_ref[2 * N + q * 2 * W:2 * N + (q + 1) * 2 * W, at] = hi

    @pl.when(has_up)
    def _():
        edge_copy(up).wait_recv()

    off = jnp.zeros((S, B), jnp.int32)
    for s in range(S):
        off = jnp.where(sub == s, off_ref[s], off)
    x = top[...]
    tau_top = jnp.where(has_up, 2.0 / (lane_sum(x * x) + EPS), 0.0)
    x = jnp.where(lane < off, x, 0.0)
    hi, lo = split(jnp.concatenate([jnp.zeros((S, B), F32), x], axis=0))
    vt[I:N, 0:B] = hi
    vt[N + I:2 * N, 0:B] = lo
    vt[2 * N + I:3 * N, 0:B] = hi
    first = gather_rows(heres, 0)
    into = [jnp.where(sub > s, lane_sum(x * row_of(heres[s], 0)), 0.0) for s in range(S)]
    meet = jnp.zeros((S, B), F32)
    tops = jnp.zeros((S, B), F32)
    for t in range(S):
        mark = (lane == I + S + t) & (sub > t)
        meet = jnp.where(mark, lane_sum(first * row_of(x, t)), meet)
        tops = jnp.where(mark, lane_sum(x * row_of(x, t)), tops)
    answer = []
    for s in range(S):
        y = jnp.where(sub == 0, row_of(meet, s), 0.0)
        for t in range(s):
            n = pair_index(s, t)
            y = jnp.where(lane == I + t, jnp.where(sub == W - 1, coef[0, n], jnp.where(sub == W - 2, coef[1, n], 0.0)), y)
        answer.append(y)
    p_m, c_m = solved(answer, B)
    a_low = gather_rows(p_m, W - 1)
    a_top = tops
    for s in range(S):
        a_top = a_top - into[s] * row_of(c_m[s], 0)
    msg[0] = a_top
    msg[1] = a_low

    v_top = jnp.concatenate([hi, lo], axis=0)

    for i, has, there in ((0, has_up, up), (1, has_down, down)):
        @pl.when(has)
        def _():
            msg_copy(i, there).start()

    for j in range(CHUNKS):
        at = pl.ds(j * width, width)
        both = jnp.dot(v_top, hi_ref[0:B, at], preferred_element_type=F32)
        acc = both[S:2 * S] + both[3 * S:] + jnp.dot(hi, lo_ref[0:B, at], preferred_element_type=F32)[S:]
        for s in range(S):
            acc = acc - wide(into[s], width) * jnp.broadcast_to(first_rows[j][s], (S, width))
        top_ref[:, at] = acc

        @pl.when(has_up)
        def _():
            sum_copy(0, j, up).start()

    k_t = []
    for s in range(S):
        x = jnp.where((lane == s * W + sub) & (sub < W - 1), 1.0, 0.0) - c_m[s]
        k_t.append(x + jnp.where((sub == W - 1) & (lane == I + s), 1.0, 0.0))
    k_t.append(jnp.zeros((S, B), F32))
    k_t.append(jnp.where(lane == I + S + sub, 1.0, 0.0))
    k_t = jnp.concatenate(k_t, axis=0)[:, :N]
    k_t = jnp.concatenate([k_t, k_t, k_t], axis=1)
    hi, lo = split(k_t)
    k_t = jnp.concatenate([hi, hi, lo], axis=0)
    y = lax.dot_general(vt[...], k_t, (((0,), (0,)), ((), ())), preferred_element_type=F32)
    hi, lo = split(y)
    spot = lax.broadcasted_iota(jnp.int32, y.shape, 1)
    y_ref[...] = jnp.where(spot < 2 * N, hi, lo)

    @pl.when(has_down)
    def _():
        msg_copy(0, down).wait_recv()

    @pl.when(has_up)
    def _():
        msg_copy(1, up).wait_recv()

    a_low = a_low + pltpu.roll(near[0], B - S, 1)
    a_top = a_top + pltpu.roll(near[1], S, 1)
    low_cols = [jnp.broadcast_to(a_low[:, I + t:I + t + 1], (S, B)) for t in range(S)]
    top_cols = [jnp.broadcast_to(a_top[:, I + S + t:I + S + t + 1], (S, B)) for t in range(S)]
    for j in range(CHUNKS):
        at = pl.ds(j * width, width)

        @pl.when(has_down)
        def _():
            sum_copy(0, j, down).wait_recv()

        @pl.when(has_up)
        def _():
            sum_copy(1, j, up).wait_recv()

        both = []
        for ref, i, tau, a in ((low_ref, 0, tau_low, low_cols), (top_ref, 1, tau_top, top_cols)):
            acc = ref[:, at] + recv[i, :, at]
            for t in range(S - 1):
                acc = acc - wide(a[t], width) * row_of(acc * wide(tau, width), t)
            both.append(acc * wide(tau, width))
        hi, lo = split(jnp.concatenate(both, axis=0))
        c_ref[I:N, at] = hi
        c_ref[N + I:2 * N, at] = lo
        c_ref[2 * N + I:3 * N, at] = hi

    for copy in sends:
        copy.wait_send()

    @pl.when(has_up)
    def _():
        msg_copy(0, up).wait_send()
        for j in range(CHUNKS):
            sum_copy(0, j, up).wait_send()

    @pl.when(has_down)
    def _():
        edge_copy(down).wait_send()
        msg_copy(1, down).wait_send()
        for j in range(CHUNKS):
            sum_copy(1, j, down).wait_send()


def second_kernel(parts, e_ref, y_ref, c_ref, o_hbm, buf, sem):
    width = buf.shape[1] // parts

    def store(j):
        at = pl.ds(pl.multiple_of(j * width, width), width)
        return pltpu.make_async_copy(buf.at[:, at], o_hbm.at[:, at], sem.at[j])

    @pl.loop(0, parts)
    def _(j):
        at = pl.ds(pl.multiple_of(j * width, width), width)
        buf[:, at] = e_ref[:, at] - jnp.dot(y_ref[...], c_ref[:, at], preferred_element_type=F32)
        store(j).start()

    @pl.loop(0, parts)
    def _(j):
        store(j).wait()


def solution(mesh):
    R, C = mesh.shape["row"], mesh.shape["col"]

    def body(vectors_in, reflectors, offsets):
        rows, cols = vectors_in.shape
        chunks = 4 if cols % 2048 == 0 else 1
        vmem = pl.BlockSpec(memory_space=pltpu.VMEM)
        anywhere = pl.BlockSpec(memory_space=pl.ANY)
        dma = pltpu.SemaphoreType.DMA
        e, y, coeff = pl.pallas_call(
            functools.partial(first_kernel, R, C, chunks),
            out_shape=(
                pltpu.VMEM((rows, cols), F32),
                pltpu.VMEM((rows, 3 * N), BF16),
                pltpu.VMEM((3 * N, cols), BF16),
            ),
            in_specs=[anywhere] * 3,
            out_specs=(vmem, vmem, vmem),
            scratch_shapes=[
                pltpu.SMEM((S,), jnp.int32),
                pltpu.VMEM(reflectors.shape, F32),
                pltpu.VMEM((W, B), F32),
                pltpu.VMEM((C, W, B), F32),
                pltpu.VMEM((rows, cols), BF16),
                pltpu.VMEM((rows, cols), BF16),
                pltpu.VMEM((3 * N, rows), BF16),
                pltpu.VMEM((3, S * (S - 1) // 2, W, B), F32),
                pltpu.VMEM((S, W, B), F32),
                pltpu.VMEM((S, B), F32),
                pltpu.VMEM((S, B), F32),
                pltpu.VMEM((S, cols), F32),
                pltpu.VMEM((S, cols), F32),
                pltpu.VMEM((2, S, B), F32),
                pltpu.VMEM((2, S, B), F32),
                pltpu.VMEM((2, S, cols), F32),
                dma, dma, dma((W,)), dma((C,)), dma((C,)), dma, dma,
                dma((2,)), dma((2,)), dma((2, chunks)), dma((2, chunks)),
            ],
            compiler_params=pltpu.CompilerParams(
                collective_id=0, has_side_effects=True, vmem_limit_bytes=24 * MIB
            ),
            name="reflect_one",
        )(
            pltpu.with_memory_space_constraint(offsets, pltpu.HBM),
            pltpu.with_memory_space_constraint(vectors_in, pltpu.HBM),
            pltpu.with_memory_space_constraint(reflectors, pltpu.HBM),
        )
        parts = max(1, cols // 256)
        return pl.pallas_call(
            functools.partial(second_kernel, parts),
            out_shape=jax.ShapeDtypeStruct((rows, cols), F32),
            in_specs=[vmem, vmem, vmem],
            out_specs=anywhere,
            scratch_shapes=[pltpu.VMEM((rows, cols), F32), dma((parts,))],
            compiler_params=pltpu.CompilerParams(vmem_limit_bytes=16 * MIB),
            name="reflect_two",
        )(*(pltpu.with_memory_space_constraint(x, pltpu.VMEM) for x in (e, y, coeff)))

    in_specs = (P("row", "col"), P(None, "row", "col"), P())
    return jax.shard_map(body, mesh=mesh, in_specs=in_specs, out_specs=P("row", "col"), check_vma=False)
```

```python
import functools

import jax
import jax.numpy as jnp
from jax import lax
from jax.experimental import pallas as pl
from jax.experimental.pallas import tpu as pltpu
from jax.sharding import PartitionSpec as P

MESH = pl.DeviceIdType.MESH
F32 = jnp.float32
BF16 = jnp.bfloat16
EPS = 1e-6
S = 8
W = 8
B = 128
I = S * W
N = I + 2 * S
EARLY = 3
MIB = 1 << 20


def split(x):
    hi = x.astype(BF16)
    return hi, (x - hi.astype(F32)).astype(BF16)


def wide(x, width):
    return jnp.concatenate([x] * (width // B), axis=1) if width > B else x


def row_of(x, i):
    return jnp.broadcast_to(x[i:i + 1], x.shape)


def gather_rows(tiles, i):
    sub = lax.broadcasted_iota(jnp.int32, tiles[0].shape, 0)
    out = jnp.zeros_like(tiles[0])
    for s, tile in enumerate(tiles):
        out = jnp.where(sub == s, row_of(tile, i), out)
    return out


def lane_sum(x):
    return jnp.broadcast_to(jnp.sum(x, axis=1, keepdims=True), x.shape)


def solve(u, own, after, before, tau, width):
    p, c, nexts, prevs = [], [], [], []
    for s in range(S):
        acc = u[s]
        for t in range(s):
            acc = acc - wide(own(s, t), width) * c[t]
            acc = acc - wide(after(s, t), width) * nexts[t]
            acc = acc - wide(before(s, t), width) * prevs[t]
        p.append(acc)
        c.append(acc * wide(tau(s), width))
        nexts.append(pltpu.roll(c[s], W - 1, 0))
        prevs.append(pltpu.roll(c[s], 1, 0))
    return p, c


def first_kernel(
    R, C, CHUNKS,
    off_hbm, e_hbm, refl_hbm,
    e_ref, y_ref, c_ref,
    off_ref, refl, mine, gat, hi_ref, lo_ref, vt, coef, fact, edge, top, low_ref, top_ref, msg, near, recv,
    off_sem, refl_sem, e_sem, out_sem, gat_sem, edge_sem, top_sem, msg_sem, near_sem, p_sem, recv_sem,
):
    r = lax.axis_index("row")
    c = lax.axis_index("col")
    up = lax.max(r - 1, 0)
    down = lax.min(r + 1, R - 1)
    has_up, has_down = r > 0, r < R - 1
    rows, cols = e_ref.shape
    step = rows // W
    width = cols // CHUNKS
    TOP = CHUNKS - 1
    piece = refl.shape[2]

    barrier = pltpu.get_barrier_semaphore()
    for d in range(1, C):
        pl.semaphore_signal(barrier, inc=1, device_id=(r, lax.rem(c + d, C)), device_id_type=MESH)

    @pl.when(has_up)
    def _():
        pl.semaphore_signal(barrier, inc=1, device_id=(up, c), device_id_type=MESH)

    @pl.when(has_down)
    def _():
        pl.semaphore_signal(barrier, inc=1, device_id=(down, c), device_id_type=MESH)

    refl_copy = pltpu.make_async_copy(refl_hbm, refl, refl_sem)
    refl_copy.start()
    off_copy = pltpu.make_async_copy(off_hbm, off_ref, off_sem)
    off_copy.start()
    loads = []
    for i in range(W):
        part = pl.ds(i * step, step)
        loads.append(pltpu.make_async_copy(e_hbm.at[part], e_ref.at[part], e_sem.at[i]))
    for load in loads[:EARLY]:
        load.start()

    refl_copy.wait()
    tile = jnp.concatenate([refl[s] for s in range(S)], axis=1)
    mine[...] = tile
    pl.semaphore_wait(barrier, C - 1 + lax.min(r, 1) + lax.min(R - 1 - r, 1))

    sends = []
    for d in sorted(range(1, C), key=lambda d: abs(d - C // 2)):
        sends.append(pltpu.make_async_remote_copy(
            src_ref=mine, dst_ref=gat.at[c], send_sem=out_sem.at[d], recv_sem=gat_sem.at[c],
            device_id=(r, lax.rem(c + d, C)), device_id_type=MESH))
    for copy in sends:
        copy.start()
    for load in loads[EARLY:]:
        load.start()
    gat[c] = tile

    def edge_copy(to):
        return pltpu.make_async_remote_copy(
            src_ref=edge, dst_ref=top, send_sem=edge_sem, recv_sem=top_sem,
            device_id=(to, c), device_id_type=MESH)

    def msg_copy(i, to):
        return pltpu.make_async_remote_copy(
            src_ref=msg.at[i], dst_ref=near.at[i], send_sem=msg_sem.at[i], recv_sem=near_sem.at[i],
            device_id=(to, c), device_id_type=MESH)

    def sum_copy(i, j, to):
        at = pl.ds(j * width, width)
        return pltpu.make_async_remote_copy(
            src_ref=(top_ref, low_ref)[i].at[:, at], dst_ref=recv.at[i, :, at],
            send_sem=p_sem.at[i, j], recv_sem=recv_sem.at[i, j],
            device_id=(to, c), device_id_type=MESH)

    @pl.when(r == 0)
    def _():
        top[...] = jnp.zeros_like(top)
        near[1] = jnp.zeros((S, B), F32)
        recv[1] = jnp.zeros((S, cols), F32)

    @pl.when(r == R - 1)
    def _():
        near[0] = jnp.zeros((S, B), F32)
        recv[0] = jnp.zeros((S, cols), F32)

    vt[...] = jnp.zeros_like(vt)

    @pl.loop(0, W)
    def _(i):
        part = pl.ds(pl.multiple_of(i * step, step), step)
        pltpu.make_async_copy(e_hbm.at[part], e_ref.at[part], e_sem.at[i]).wait()
        hi, lo = split(e_ref[part])
        hi_ref[part] = hi
        lo_ref[part] = lo

    off_copy.wait()
    lane = lax.broadcasted_iota(jnp.int32, (S, B), 1)
    sub = lax.broadcasted_iota(jnp.int32, (S, B), 0)

    for d in range(1, C):
        src = lax.rem(c + d, C)
        pltpu.make_async_remote_copy(
            src_ref=mine, dst_ref=gat.at[src], send_sem=out_sem.at[d], recv_sem=gat_sem.at[src],
            device_id=(r, src), device_id_type=MESH).wait_recv()

    parts = [gat[q] for q in range(C)]
    turned, heres, overs, taus = [], [], [], []
    for s in range(S):
        x = jnp.zeros((W, B), F32)
        for q in range(C):
            turn = ((q - s) * piece) % B
            y = parts[q] if turn == 0 else pltpu.roll(parts[q], turn, 1)
            x = jnp.where((lane >= q * piece) & (lane < (q + 1) * piece), y, x)
        o = off_ref[s]
        turned.append(pltpu.roll(x, o, 1))
    edge[...] = gather_rows(turned, W - 1)

    @pl.when(has_down)
    def _():
        edge_copy(down).start()

    for s in range(S):
        x, o = turned[s], off_ref[s]
        here = jnp.where(lane >= o, x, 0.0)
        over = jnp.where(lane < o, x, 0.0)
        whole = here * here + jnp.where((sub < W - 1) | has_down, over * over, 0.0)
        taus.append(2.0 / (lane_sum(whole) + EPS))
        over = jnp.where(sub < W - 1, over, 0.0)
        heres.append(here)
        overs.append(over)
        fact[s] = jnp.where(sub < W - 1, taus[s], 0.0)
    tau_low = gather_rows(taus, W - 1)
    for q in range(S // 2):
        for t in range(W):
            pair = []
            for s in (2 * q, 2 * q + 1):
                x = jnp.where(sub == t, heres[s], 0.0)
                if t > 0:
                    x = x + jnp.where(sub == t - 1, overs[s], 0.0)
                pair.append(x)
            hi, lo = split(jnp.concatenate(pair, axis=0))
            at = pl.ds(t * B, B)
            vt[q * 2 * W:(q + 1) * 2 * W, at] = hi
            vt[N + q * 2 * W:N + (q + 1) * 2 * W, at] = lo
            vt[2 * N + q * 2 * W:2 * N + (q + 1) * 2 * W, at] = hi

    def pair_index(s, t):
        return s * (s - 1) // 2 + t

    for s in range(S):
        for t in range(s):
            own = lane_sum(heres[s] * heres[t] + overs[s] * overs[t])
            after = lane_sum(overs[s] * pltpu.roll(heres[t], W - 1, 0))
            before = lane_sum(heres[s] * pltpu.roll(overs[t], 1, 0))
            n = pair_index(s, t)
            coef[0, n] = own
            coef[1, n] = after
            coef[2, n] = before

    def solved(u, w):
        return solve(
            u, lambda s, t: coef[0, pair_index(s, t)], lambda s, t: coef[1, pair_index(s, t)],
            lambda s, t: coef[2, pair_index(s, t)], lambda s: fact[s], w)

    def top_part():
        @pl.when(has_up)
        def _():
            edge_copy(up).wait_recv()

        off = jnp.zeros((S, B), jnp.int32)
        for s in range(S):
            off = jnp.where(sub == s, off_ref[s], off)
        x = top[...]
        tau_top = jnp.where(has_up, 2.0 / (lane_sum(x * x) + EPS), 0.0)
        x = jnp.where(lane < off, x, 0.0)
        hi, lo = split(jnp.concatenate([jnp.zeros((S, B), F32), x], axis=0))
        vt[I:N, 0:B] = hi
        vt[N + I:2 * N, 0:B] = lo
        vt[2 * N + I:3 * N, 0:B] = hi
        first = gather_rows(heres, 0)
        into = [jnp.where(sub > s, lane_sum(x * row_of(heres[s], 0)), 0.0) for s in range(S)]
        meet = jnp.zeros((S, B), F32)
        tops = jnp.zeros((S, B), F32)
        for t in range(S):
            mark = (lane == I + S + t) & (sub > t)
            meet = jnp.where(mark, lane_sum(first * row_of(x, t)), meet)
            tops = jnp.where(mark, lane_sum(x * row_of(x, t)), tops)
        answer = []
        for s in range(S):
            y = jnp.where(sub == 0, row_of(meet, s), 0.0)
            for t in range(s):
                n = pair_index(s, t)
                y = jnp.where(lane == I + t, jnp.where(sub == W - 1, coef[0, n], jnp.where(sub == W - 2, coef[1, n], 0.0)), y)
            answer.append(y)
        p_m, c_m = solved(answer, B)
        a_low = gather_rows(p_m, W - 1)
        a_top = tops
        for s in range(S):
            a_top = a_top - into[s] * row_of(c_m[s], 0)
        msg[0] = a_top
        msg[1] = a_low

        v_top = jnp.concatenate([hi, lo], axis=0)

        for i, has, there in ((0, has_up, up), (1, has_down, down)):
            @pl.when(has)
            def _():
                msg_copy(i, there).start()
        return v_top, into, tau_top, a_top, a_low, c_m

    def top_sums(j):
        at = pl.ds(j * width, width)
        both = jnp.dot(v_top, hi_ref[0:B, at], preferred_element_type=F32)
        acc = both[S:2 * S] + both[3 * S:] + jnp.dot(v_top[:2 * S], lo_ref[0:B, at], preferred_element_type=F32)[S:]
        for s in range(S):
            acc = acc - wide(into[s], width) * jnp.broadcast_to(first_rows[j][s], (S, width))
        top_ref[:, at] = acc

        @pl.when(has_up)
        def _():
            sum_copy(0, j, up).start()

    first_rows = []
    for j in range(CHUNKS):
        at = pl.ds(j * width, width)
        both = jnp.dot(vt[0:2 * N, :], hi_ref[:, at], preferred_element_type=F32)
        u = both[:I] + both[N:N + I] + jnp.dot(vt[0:I, :], lo_ref[:, at], preferred_element_type=F32)
        p, cs = solved([u[s * W:(s + 1) * W] for s in range(S)], width)
        low_ref[:, at] = gather_rows(p, W - 1)

        @pl.when(has_down)
        def _():
            sum_copy(1, j, down).start()

        first_rows.append([x[0:1] for x in cs])
        for q in range(S // 2):
            hi, lo = split(jnp.concatenate(cs[2 * q:2 * q + 2], axis=0))
            c_ref[q * 2 * W:(q + 1) * 2 * W, at] = hi
            c_ref[N + q * 2 * W:N + (q + 1) * 2 * W, at] = lo
            c_ref[2 * N + q * 2 * W:2 * N + (q + 1) * 2 * W, at] = hi

        if j == TOP:
            v_top, into, tau_top, a_top, a_low, c_m = top_part()
            for i in range(j):
                top_sums(i)
        if j >= TOP:
            top_sums(j)

    k_t = []
    for s in range(S):
        x = jnp.where((lane == s * W + sub) & (sub < W - 1), 1.0, 0.0) - c_m[s]
        k_t.append(x + jnp.where((sub == W - 1) & (lane == I + s), 1.0, 0.0))
    k_t.append(jnp.zeros((S, B), F32))
    k_t.append(jnp.where(lane == I + S + sub, 1.0, 0.0))
    k_t = jnp.concatenate(k_t, axis=0)[:, :N]
    k_t = jnp.concatenate([k_t, k_t, k_t], axis=1)
    hi, lo = split(k_t)
    k_t = jnp.concatenate([hi, hi, lo], axis=0)
    y = lax.dot_general(vt[...], k_t, (((0,), (0,)), ((), ())), preferred_element_type=F32)
    hi, lo = split(y)
    spot = lax.broadcasted_iota(jnp.int32, y.shape, 1)
    y_ref[...] = jnp.where(spot < 2 * N, hi, lo)

    @pl.when(has_down)
    def _():
        msg_copy(0, down).wait_recv()

    @pl.when(has_up)
    def _():
        msg_copy(1, up).wait_recv()

    a_low = a_low + pltpu.roll(near[0], B - S, 1)
    a_top = a_top + pltpu.roll(near[1], S, 1)
    low_cols = [jnp.broadcast_to(a_low[:, I + t:I + t + 1], (S, B)) for t in range(S)]
    top_cols = [jnp.broadcast_to(a_top[:, I + S + t:I + S + t + 1], (S, B)) for t in range(S)]
    for j in range(CHUNKS):
        at = pl.ds(j * width, width)

        @pl.when(has_down)
        def _():
            sum_copy(0, j, down).wait_recv()

        @pl.when(has_up)
        def _():
            sum_copy(1, j, up).wait_recv()

        both = []
        for ref, i, tau, a in ((low_ref, 0, tau_low, low_cols), (top_ref, 1, tau_top, top_cols)):
            acc = ref[:, at] + recv[i, :, at]
            for t in range(S - 1):
                acc = acc - wide(a[t], width) * row_of(acc * wide(tau, width), t)
            both.append(acc * wide(tau, width))
        hi, lo = split(jnp.concatenate(both, axis=0))
        c_ref[I:N, at] = hi
        c_ref[N + I:2 * N, at] = lo
        c_ref[2 * N + I:3 * N, at] = hi

    for copy in sends:
        copy.wait_send()

    @pl.when(has_up)
    def _():
        msg_copy(0, up).wait_send()
        for j in range(CHUNKS):
            sum_copy(0, j, up).wait_send()

    @pl.when(has_down)
    def _():
        edge_copy(down).wait_send()
        msg_copy(1, down).wait_send()
        for j in range(CHUNKS):
            sum_copy(1, j, down).wait_send()


def second_kernel(parts, e_ref, y_ref, c_ref, o_hbm, buf, sem):
    width = buf.shape[1] // parts

    def store(j):
        at = pl.ds(pl.multiple_of(j * width, width), width)
        return pltpu.make_async_copy(buf.at[:, at], o_hbm.at[:, at], sem.at[j])

    @pl.loop(0, parts)
    def _(j):
        at = pl.ds(pl.multiple_of(j * width, width), width)
        buf[:, at] = e_ref[:, at] - jnp.dot(y_ref[...], c_ref[:, at], preferred_element_type=F32)
        store(j).start()

    @pl.loop(0, parts)
    def _(j):
        store(j).wait()


def solution(mesh):
    R, C = mesh.shape["row"], mesh.shape["col"]

    def body(vectors_in, reflectors, offsets):
        rows, cols = vectors_in.shape
        chunks = 4 if cols % 2048 == 0 else 1
        vmem = pl.BlockSpec(memory_space=pltpu.VMEM)
        anywhere = pl.BlockSpec(memory_space=pl.ANY)
        dma = pltpu.SemaphoreType.DMA
        e, y, coeff = pl.pallas_call(
            functools.partial(first_kernel, R, C, chunks),
            out_shape=(
                pltpu.VMEM((rows, cols), F32),
                pltpu.VMEM((rows, 3 * N), BF16),
                pltpu.VMEM((3 * N, cols), BF16),
            ),
            in_specs=[anywhere] * 3,
            out_specs=(vmem, vmem, vmem),
            scratch_shapes=[
                pltpu.SMEM((S,), jnp.int32),
                pltpu.VMEM(reflectors.shape, F32),
                pltpu.VMEM((W, B), F32),
                pltpu.VMEM((C, W, B), F32),
                pltpu.VMEM((rows, cols), BF16),
                pltpu.VMEM((rows, cols), BF16),
                pltpu.VMEM((3 * N, rows), BF16),
                pltpu.VMEM((3, S * (S - 1) // 2, W, B), F32),
                pltpu.VMEM((S, W, B), F32),
                pltpu.VMEM((S, B), F32),
                pltpu.VMEM((S, B), F32),
                pltpu.VMEM((S, cols), F32),
                pltpu.VMEM((S, cols), F32),
                pltpu.VMEM((2, S, B), F32),
                pltpu.VMEM((2, S, B), F32),
                pltpu.VMEM((2, S, cols), F32),
                dma, dma, dma((W,)), dma((C,)), dma((C,)), dma, dma,
                dma((2,)), dma((2,)), dma((2, chunks)), dma((2, chunks)),
            ],
            compiler_params=pltpu.CompilerParams(
                collective_id=0, has_side_effects=True, vmem_limit_bytes=24 * MIB
            ),
            name="reflect_one",
        )(
            pltpu.with_memory_space_constraint(offsets, pltpu.HBM),
            pltpu.with_memory_space_constraint(vectors_in, pltpu.HBM),
            pltpu.with_memory_space_constraint(reflectors, pltpu.HBM),
        )
        parts = max(1, cols // 256)
        return pl.pallas_call(
            functools.partial(second_kernel, parts),
            out_shape=jax.ShapeDtypeStruct((rows, cols), F32),
            in_specs=[vmem, vmem, vmem],
            out_specs=anywhere,
            scratch_shapes=[pltpu.VMEM((rows, cols), F32), dma((parts,))],
            compiler_params=pltpu.CompilerParams(vmem_limit_bytes=16 * MIB),
            name="reflect_two",
        )(*(pltpu.with_memory_space_constraint(x, pltpu.VMEM) for x in (e, y, coeff)))

    in_specs = (P("row", "col"), P(None, "row", "col"), P())
    return jax.shard_map(body, mesh=mesh, in_specs=in_specs, out_specs=P("row", "col"), check_vma=False)
```

```python
import functools

import jax
import jax.numpy as jnp
from jax import lax
from jax.experimental import pallas as pl
from jax.experimental.pallas import tpu as pltpu
from jax.sharding import PartitionSpec as P

MESH = pl.DeviceIdType.MESH
F32 = jnp.float32
BF16 = jnp.bfloat16
EPS = 1e-6
S = 8
W = 8
B = 128
I = S * W
N = I + 2 * S
EARLY = 3
MIB = 1 << 20


def split(x):
    hi = x.astype(BF16)
    return hi, (x - hi.astype(F32)).astype(BF16)


def wide(x, width):
    return jnp.concatenate([x] * (width // B), axis=1) if width > B else x


def row_of(x, i):
    return jnp.broadcast_to(x[i:i + 1], x.shape)


def gather_rows(tiles, i):
    sub = lax.broadcasted_iota(jnp.int32, tiles[0].shape, 0)
    out = jnp.zeros_like(tiles[0])
    for s, tile in enumerate(tiles):
        out = jnp.where(sub == s, row_of(tile, i), out)
    return out


def lane_sum(x):
    return jnp.broadcast_to(jnp.sum(x, axis=1, keepdims=True), x.shape)


def solve(u, own, after, before, tau, width):
    p, c, nexts, prevs = [], [], [], []
    for s in range(S):
        acc = u[s]
        for t in range(s):
            acc = acc - wide(own(s, t), width) * c[t]
            acc = acc - wide(after(s, t), width) * nexts[t]
            acc = acc - wide(before(s, t), width) * prevs[t]
        p.append(acc)
        c.append(acc * wide(tau(s), width))
        nexts.append(pltpu.roll(c[s], W - 1, 0))
        prevs.append(pltpu.roll(c[s], 1, 0))
    return p, c


def first_kernel(
    R, C, CHUNKS,
    off_hbm, e_hbm, refl_hbm,
    e_ref, y_ref, c_ref,
    off_ref, refl, mine, gat, hi_ref, lo_ref, vt, coef, fact, edge, top, low_ref, top_ref, msg, near, recv,
    off_sem, refl_sem, e_sem, out_sem, gat_sem, edge_sem, top_sem, msg_sem, near_sem, p_sem, recv_sem,
):
    r = lax.axis_index("row")
    c = lax.axis_index("col")
    up = lax.max(r - 1, 0)
    down = lax.min(r + 1, R - 1)
    has_up, has_down = r > 0, r < R - 1
    rows, cols = e_ref.shape
    step = rows // W
    width = cols // CHUNKS
    TOP = CHUNKS - 1
    piece = refl.shape[2]

    barrier = pltpu.get_barrier_semaphore()
    for d in range(1, C):
        pl.semaphore_signal(barrier, inc=1, device_id=(r, lax.rem(c + d, C)), device_id_type=MESH)

    @pl.when(has_up)
    def _():
        pl.semaphore_signal(barrier, inc=1, device_id=(up, c), device_id_type=MESH)

    @pl.when(has_down)
    def _():
        pl.semaphore_signal(barrier, inc=1, device_id=(down, c), device_id_type=MESH)

    refl_copy = pltpu.make_async_copy(refl_hbm, refl, refl_sem)
    refl_copy.start()
    off_copy = pltpu.make_async_copy(off_hbm, off_ref, off_sem)
    off_copy.start()
    loads = []
    for i in range(W):
        part = pl.ds(i * step, step)
        loads.append(pltpu.make_async_copy(e_hbm.at[part], e_ref.at[part], e_sem.at[i]))
    for load in loads[:EARLY]:
        load.start()

    refl_copy.wait()
    tile = jnp.concatenate([refl[s] for s in range(S)], axis=1)
    mine[...] = tile
    pl.semaphore_wait(barrier, C - 1 + lax.min(r, 1) + lax.min(R - 1 - r, 1))

    sends = []
    for d in sorted(range(1, C), key=lambda d: abs(d - C // 2)):
        sends.append(pltpu.make_async_remote_copy(
            src_ref=mine, dst_ref=gat.at[c], send_sem=out_sem.at[d], recv_sem=gat_sem.at[c],
            device_id=(r, lax.rem(c + d, C)), device_id_type=MESH))
    for copy in sends:
        copy.start()
    for load in loads[EARLY:]:
        load.start()
    gat[c] = tile

    def edge_copy(to):
        return pltpu.make_async_remote_copy(
            src_ref=edge, dst_ref=top, send_sem=edge_sem, recv_sem=top_sem,
            device_id=(to, c), device_id_type=MESH)

    def msg_copy(i, to):
        return pltpu.make_async_remote_copy(
            src_ref=msg.at[i], dst_ref=near.at[i], send_sem=msg_sem.at[i], recv_sem=near_sem.at[i],
            device_id=(to, c), device_id_type=MESH)

    def sum_copy(i, j, to):
        at = pl.ds(j * width, width)
        return pltpu.make_async_remote_copy(
            src_ref=(top_ref, low_ref)[i].at[:, at], dst_ref=recv.at[i, :, at],
            send_sem=p_sem.at[i, j], recv_sem=recv_sem.at[i, j],
            device_id=(to, c), device_id_type=MESH)

    @pl.when(r == 0)
    def _():
        top[...] = jnp.zeros_like(top)
        near[1] = jnp.zeros((S, B), F32)
        recv[1] = jnp.zeros((S, cols), F32)

    @pl.when(r == R - 1)
    def _():
        near[0] = jnp.zeros((S, B), F32)
        recv[0] = jnp.zeros((S, cols), F32)

    vt[...] = jnp.zeros_like(vt)

    @pl.loop(0, W)
    def _(i):
        part = pl.ds(pl.multiple_of(i * step, step), step)
        pltpu.make_async_copy(e_hbm.at[part], e_ref.at[part], e_sem.at[i]).wait()
        hi, lo = split(e_ref[part])
        hi_ref[part] = hi
        lo_ref[part] = lo

    off_copy.wait()
    lane = lax.broadcasted_iota(jnp.int32, (S, B), 1)
    sub = lax.broadcasted_iota(jnp.int32, (S, B), 0)

    for d in range(1, C):
        src = lax.rem(c + d, C)
        pltpu.make_async_remote_copy(
            src_ref=mine, dst_ref=gat.at[src], send_sem=out_sem.at[d], recv_sem=gat_sem.at[src],
            device_id=(r, src), device_id_type=MESH).wait_recv()

    parts = [gat[q] for q in range(C)]
    blocks = [(lane >= q * piece) & (lane < (q + 1) * piece) for q in range(C)]

    def pick(tiles):
        out = tiles[0]
        for q in range(1, C):
            out = jnp.where(blocks[q], tiles[q], out)
        return out

    moved = []
    for d in range(C):
        y = pick([parts[(s + d) % C] for s in range(S)])
        moved.append(y if d == 0 else pltpu.roll(y, d * piece, 1))
    turned, heres, overs, taus = [], [], [], []
    for s in range(S):
        x = pick([moved[(q - s) % C] for q in range(C)])
        o = off_ref[s]
        turned.append(pltpu.roll(x, o, 1))
    edge[...] = gather_rows(turned, W - 1)

    @pl.when(has_down)
    def _():
        edge_copy(down).start()

    for s in range(S):
        x, o = turned[s], off_ref[s]
        here = jnp.where(lane >= o, x, 0.0)
        over = jnp.where(lane < o, x, 0.0)
        whole = here * here + jnp.where((sub < W - 1) | has_down, over * over, 0.0)
        taus.append(2.0 / (lane_sum(whole) + EPS))
        over = jnp.where(sub < W - 1, over, 0.0)
        heres.append(here)
        overs.append(over)
        fact[s] = jnp.where(sub < W - 1, taus[s], 0.0)
    tau_low = gather_rows(taus, W - 1)
    for q in range(S // 2):
        for t in range(W):
            pair = []
            for s in (2 * q, 2 * q + 1):
                x = jnp.where(sub == t, heres[s], 0.0)
                if t > 0:
                    x = x + jnp.where(sub == t - 1, overs[s], 0.0)
                pair.append(x)
            hi, lo = split(jnp.concatenate(pair, axis=0))
            at = pl.ds(t * B, B)
            vt[q * 2 * W:(q + 1) * 2 * W, at] = hi
            vt[N + q * 2 * W:N + (q + 1) * 2 * W, at] = lo
            vt[2 * N + q * 2 * W:2 * N + (q + 1) * 2 * W, at] = hi

    def pair_index(s, t):
        return s * (s - 1) // 2 + t

    for s in range(S):
        for t in range(s):
            own = lane_sum(heres[s] * heres[t] + overs[s] * overs[t])
            after = lane_sum(overs[s] * pltpu.roll(heres[t], W - 1, 0))
            before = lane_sum(heres[s] * pltpu.roll(overs[t], 1, 0))
            n = pair_index(s, t)
            coef[0, n] = own
            coef[1, n] = after
            coef[2, n] = before

    def solved(u, w):
        return solve(
            u, lambda s, t: coef[0, pair_index(s, t)], lambda s, t: coef[1, pair_index(s, t)],
            lambda s, t: coef[2, pair_index(s, t)], lambda s: fact[s], w)

    def top_part():
        @pl.when(has_up)
        def _():
            edge_copy(up).wait_recv()

        off = jnp.zeros((S, B), jnp.int32)
        for s in range(S):
            off = jnp.where(sub == s, off_ref[s], off)
        x = top[...]
        tau_top = jnp.where(has_up, 2.0 / (lane_sum(x * x) + EPS), 0.0)
        x = jnp.where(lane < off, x, 0.0)
        hi, lo = split(jnp.concatenate([jnp.zeros((S, B), F32), x], axis=0))
        vt[I:N, 0:B] = hi
        vt[N + I:2 * N, 0:B] = lo
        vt[2 * N + I:3 * N, 0:B] = hi
        first = gather_rows(heres, 0)
        into = [jnp.where(sub > s, lane_sum(x * row_of(heres[s], 0)), 0.0) for s in range(S)]
        meet = jnp.zeros((S, B), F32)
        tops = jnp.zeros((S, B), F32)
        for t in range(S):
            mark = (lane == I + S + t) & (sub > t)
            meet = jnp.where(mark, lane_sum(first * row_of(x, t)), meet)
            tops = jnp.where(mark, lane_sum(x * row_of(x, t)), tops)
        answer = []
        for s in range(S):
            y = jnp.where(sub == 0, row_of(meet, s), 0.0)
            for t in range(s):
                n = pair_index(s, t)
                y = jnp.where(lane == I + t, jnp.where(sub == W - 1, coef[0, n], jnp.where(sub == W - 2, coef[1, n], 0.0)), y)
            answer.append(y)
        p_m, c_m = solved(answer, B)
        a_low = gather_rows(p_m, W - 1)
        a_top = tops
        for s in range(S):
            a_top = a_top - into[s] * row_of(c_m[s], 0)
        msg[0] = a_top
        msg[1] = a_low

        v_top = jnp.concatenate([hi, lo], axis=0)

        for i, has, there in ((0, has_up, up), (1, has_down, down)):
            @pl.when(has)
            def _():
                msg_copy(i, there).start()
        return v_top, into, tau_top, a_top, a_low, c_m

    def top_sums(j):
        at = pl.ds(j * width, width)
        both = jnp.dot(v_top, hi_ref[0:B, at], preferred_element_type=F32)
        acc = both[S:2 * S] + both[3 * S:] + jnp.dot(v_top[:2 * S], lo_ref[0:B, at], preferred_element_type=F32)[S:]
        for s in range(S):
            acc = acc - wide(into[s], width) * jnp.broadcast_to(first_rows[j][s], (S, width))
        top_ref[:, at] = acc

        @pl.when(has_up)
        def _():
            sum_copy(0, j, up).start()

    first_rows = []
    for j in range(CHUNKS):
        at = pl.ds(j * width, width)
        both = jnp.dot(vt[0:2 * N, :], hi_ref[:, at], preferred_element_type=F32)
        u = both[:I] + both[N:N + I] + jnp.dot(vt[0:I, :], lo_ref[:, at], preferred_element_type=F32)
        p, cs = solved([u[s * W:(s + 1) * W] for s in range(S)], width)
        low_ref[:, at] = gather_rows(p, W - 1)

        @pl.when(has_down)
        def _():
            sum_copy(1, j, down).start()

        first_rows.append([x[0:1] for x in cs])
        for q in range(S // 2):
            hi, lo = split(jnp.concatenate(cs[2 * q:2 * q + 2], axis=0))
            c_ref[q * 2 * W:(q + 1) * 2 * W, at] = hi
            c_ref[N + q * 2 * W:N + (q + 1) * 2 * W, at] = lo
            c_ref[2 * N + q * 2 * W:2 * N + (q + 1) * 2 * W, at] = hi

        if j == TOP:
            v_top, into, tau_top, a_top, a_low, c_m = top_part()
            for i in range(j):
                top_sums(i)
        if j >= TOP:
            top_sums(j)

    k_t = []
    for s in range(S):
        x = jnp.where((lane == s * W + sub) & (sub < W - 1), 1.0, 0.0) - c_m[s]
        k_t.append(x + jnp.where((sub == W - 1) & (lane == I + s), 1.0, 0.0))
    k_t.append(jnp.zeros((S, B), F32))
    k_t.append(jnp.where(lane == I + S + sub, 1.0, 0.0))
    k_t = jnp.concatenate(k_t, axis=0)[:, :N]
    k_t = jnp.concatenate([k_t, k_t, k_t], axis=1)
    hi, lo = split(k_t)
    k_t = jnp.concatenate([hi, hi, lo], axis=0)
    y = lax.dot_general(vt[...], k_t, (((0,), (0,)), ((), ())), preferred_element_type=F32)
    hi, lo = split(y)
    spot = lax.broadcasted_iota(jnp.int32, y.shape, 1)
    y_ref[...] = jnp.where(spot < 2 * N, hi, lo)

    @pl.when(has_down)
    def _():
        msg_copy(0, down).wait_recv()

    @pl.when(has_up)
    def _():
        msg_copy(1, up).wait_recv()

    a_low = a_low + pltpu.roll(near[0], B - S, 1)
    a_top = a_top + pltpu.roll(near[1], S, 1)
    low_cols = [jnp.broadcast_to(a_low[:, I + t:I + t + 1], (S, B)) for t in range(S)]
    top_cols = [jnp.broadcast_to(a_top[:, I + S + t:I + S + t + 1], (S, B)) for t in range(S)]
    for j in range(CHUNKS):
        at = pl.ds(j * width, width)

        @pl.when(has_down)
        def _():
            sum_copy(0, j, down).wait_recv()

        @pl.when(has_up)
        def _():
            sum_copy(1, j, up).wait_recv()

        both = []
        for ref, i, tau, a in ((low_ref, 0, tau_low, low_cols), (top_ref, 1, tau_top, top_cols)):
            acc = ref[:, at] + recv[i, :, at]
            for t in range(S - 1):
                acc = acc - wide(a[t], width) * row_of(acc * wide(tau, width), t)
            both.append(acc * wide(tau, width))
        hi, lo = split(jnp.concatenate(both, axis=0))
        c_ref[I:N, at] = hi
        c_ref[N + I:2 * N, at] = lo
        c_ref[2 * N + I:3 * N, at] = hi

    for copy in sends:
        copy.wait_send()

    @pl.when(has_up)
    def _():
        msg_copy(0, up).wait_send()
        for j in range(CHUNKS):
            sum_copy(0, j, up).wait_send()

    @pl.when(has_down)
    def _():
        edge_copy(down).wait_send()
        msg_copy(1, down).wait_send()
        for j in range(CHUNKS):
            sum_copy(1, j, down).wait_send()


def second_kernel(parts, e_ref, y_ref, c_ref, o_hbm, buf, sem):
    width = buf.shape[1] // parts

    def store(j):
        at = pl.ds(pl.multiple_of(j * width, width), width)
        return pltpu.make_async_copy(buf.at[:, at], o_hbm.at[:, at], sem.at[j])

    @pl.loop(0, parts)
    def _(j):
        at = pl.ds(pl.multiple_of(j * width, width), width)
        buf[:, at] = e_ref[:, at] - jnp.dot(y_ref[...], c_ref[:, at], preferred_element_type=F32)
        store(j).start()

    @pl.loop(0, parts)
    def _(j):
        store(j).wait()


def solution(mesh):
    R, C = mesh.shape["row"], mesh.shape["col"]

    def body(vectors_in, reflectors, offsets):
        rows, cols = vectors_in.shape
        chunks = 2 if cols % 2048 == 0 else 1
        vmem = pl.BlockSpec(memory_space=pltpu.VMEM)
        anywhere = pl.BlockSpec(memory_space=pl.ANY)
        dma = pltpu.SemaphoreType.DMA
        e, y, coeff = pl.pallas_call(
            functools.partial(first_kernel, R, C, chunks),
            out_shape=(
                pltpu.VMEM((rows, cols), F32),
                pltpu.VMEM((rows, 3 * N), BF16),
                pltpu.VMEM((3 * N, cols), BF16),
            ),
            in_specs=[anywhere] * 3,
            out_specs=(vmem, vmem, vmem),
            scratch_shapes=[
                pltpu.SMEM((S,), jnp.int32),
                pltpu.VMEM(reflectors.shape, F32),
                pltpu.VMEM((W, B), F32),
                pltpu.VMEM((C, W, B), F32),
                pltpu.VMEM((rows, cols), BF16),
                pltpu.VMEM((rows, cols), BF16),
                pltpu.VMEM((3 * N, rows), BF16),
                pltpu.VMEM((3, S * (S - 1) // 2, W, B), F32),
                pltpu.VMEM((S, W, B), F32),
                pltpu.VMEM((S, B), F32),
                pltpu.VMEM((S, B), F32),
                pltpu.VMEM((S, cols), F32),
                pltpu.VMEM((S, cols), F32),
                pltpu.VMEM((2, S, B), F32),
                pltpu.VMEM((2, S, B), F32),
                pltpu.VMEM((2, S, cols), F32),
                dma, dma, dma((W,)), dma((C,)), dma((C,)), dma, dma,
                dma((2,)), dma((2,)), dma((2, chunks)), dma((2, chunks)),
            ],
            compiler_params=pltpu.CompilerParams(
                collective_id=0, has_side_effects=True, vmem_limit_bytes=24 * MIB
            ),
            name="reflect_one",
        )(
            pltpu.with_memory_space_constraint(offsets, pltpu.HBM),
            pltpu.with_memory_space_constraint(vectors_in, pltpu.HBM),
            pltpu.with_memory_space_constraint(reflectors, pltpu.HBM),
        )
        parts = max(1, cols // 256)
        return pl.pallas_call(
            functools.partial(second_kernel, parts),
            out_shape=jax.ShapeDtypeStruct((rows, cols), F32),
            in_specs=[vmem, vmem, vmem],
            out_specs=anywhere,
            scratch_shapes=[pltpu.VMEM((rows, cols), F32), dma((parts,))],
            compiler_params=pltpu.CompilerParams(vmem_limit_bytes=16 * MIB),
            name="reflect_two",
        )(*(pltpu.with_memory_space_constraint(x, pltpu.VMEM) for x in (e, y, coeff)))

    in_specs = (P("row", "col"), P(None, "row", "col"), P())
    return jax.shard_map(body, mesh=mesh, in_specs=in_specs, out_specs=P("row", "col"), check_vma=False)
```

```python
import functools

import jax
import jax.numpy as jnp
from jax import lax
from jax.experimental import pallas as pl
from jax.experimental.pallas import tpu as pltpu
from jax.sharding import PartitionSpec as P

MESH = pl.DeviceIdType.MESH
F32 = jnp.float32
BF16 = jnp.bfloat16
EPS = 1e-6
S = 8
W = 8
B = 128
I = S * W
N = I + 2 * S
LOADS = 4
EARLY = 2
MIB = 1 << 20


def split(x):
    hi = x.astype(BF16)
    return hi, (x - hi.astype(F32)).astype(BF16)


def wide(x, width):
    return jnp.concatenate([x] * (width // B), axis=1) if width > B else x


def row_of(x, i):
    return jnp.broadcast_to(x[i:i + 1], x.shape)


def gather_rows(tiles, i):
    sub = lax.broadcasted_iota(jnp.int32, tiles[0].shape, 0)
    out = jnp.zeros_like(tiles[0])
    for s, tile in enumerate(tiles):
        out = jnp.where(sub == s, row_of(tile, i), out)
    return out


def lane_sum(x):
    return jnp.broadcast_to(jnp.sum(x, axis=1, keepdims=True), x.shape)


def solve(u, own, after, before, tau, width):
    p, c, nexts, prevs = [], [], [], []
    for s in range(S):
        acc = u[s]
        for t in range(s):
            acc = acc - wide(own(s, t), width) * c[t]
            acc = acc - wide(after(s, t), width) * nexts[t]
            acc = acc - wide(before(s, t), width) * prevs[t]
        p.append(acc)
        c.append(acc * wide(tau(s), width))
        nexts.append(pltpu.roll(c[s], W - 1, 0))
        prevs.append(pltpu.roll(c[s], 1, 0))
    return p, c


def first_kernel(
    R, C, CHUNKS,
    off_hbm, e_hbm, refl_hbm,
    e_ref, y_ref, c_ref,
    off_ref, refl, mine, gat, hi_ref, lo_ref, vt, coef, fact, edge, top, low_ref, top_ref, msg, near, recv,
    off_sem, refl_sem, e_sem, out_sem, gat_sem, edge_sem, top_sem, msg_sem, near_sem, p_sem, recv_sem,
):
    r = lax.axis_index("row")
    c = lax.axis_index("col")
    up = lax.max(r - 1, 0)
    down = lax.min(r + 1, R - 1)
    has_up, has_down = r > 0, r < R - 1
    rows, cols = e_ref.shape
    step = rows // LOADS
    width = cols // CHUNKS
    TOP = CHUNKS - 1
    piece = refl.shape[2]

    barrier = pltpu.get_barrier_semaphore()
    for d in range(1, C):
        pl.semaphore_signal(barrier, inc=1, device_id=(r, lax.rem(c + d, C)), device_id_type=MESH)

    @pl.when(has_up)
    def _():
        pl.semaphore_signal(barrier, inc=1, device_id=(up, c), device_id_type=MESH)

    @pl.when(has_down)
    def _():
        pl.semaphore_signal(barrier, inc=1, device_id=(down, c), device_id_type=MESH)

    refl_copy = pltpu.make_async_copy(refl_hbm, refl, refl_sem)
    refl_copy.start()
    off_copy = pltpu.make_async_copy(off_hbm, off_ref, off_sem)
    off_copy.start()
    loads = []
    for i in range(LOADS):
        part = pl.ds(i * step, step)
        loads.append(pltpu.make_async_copy(e_hbm.at[part], e_ref.at[part], e_sem.at[i]))
    for load in loads[:EARLY]:
        load.start()

    refl_copy.wait()
    tile = jnp.concatenate([refl[s] for s in range(S)], axis=1)
    mine[...] = tile
    pl.semaphore_wait(barrier, C - 1 + lax.min(r, 1) + lax.min(R - 1 - r, 1))

    sends = []
    for d in sorted(range(1, C), key=lambda d: abs(d - C // 2)):
        sends.append(pltpu.make_async_remote_copy(
            src_ref=mine, dst_ref=gat.at[c], send_sem=out_sem, recv_sem=gat_sem,
            device_id=(r, lax.rem(c + d, C)), device_id_type=MESH))
    for copy in sends:
        copy.start()
    for load in loads[EARLY:]:
        load.start()
    gat[c] = tile

    def edge_copy(to):
        return pltpu.make_async_remote_copy(
            src_ref=edge, dst_ref=top, send_sem=edge_sem, recv_sem=top_sem,
            device_id=(to, c), device_id_type=MESH)

    def msg_copy(i, to):
        return pltpu.make_async_remote_copy(
            src_ref=msg.at[i], dst_ref=near.at[i], send_sem=msg_sem.at[i], recv_sem=near_sem.at[i],
            device_id=(to, c), device_id_type=MESH)

    def sum_copy(i, j, to):
        at = pl.ds(j * width, width)
        return pltpu.make_async_remote_copy(
            src_ref=(top_ref, low_ref)[i].at[:, at], dst_ref=recv.at[i, :, at],
            send_sem=p_sem.at[i], recv_sem=recv_sem.at[i, j],
            device_id=(to, c), device_id_type=MESH)

    def sums_sent(i, to):
        return pltpu.make_async_remote_copy(
            src_ref=(top_ref, low_ref)[i], dst_ref=recv.at[i], send_sem=p_sem.at[i], recv_sem=recv_sem.at[i, 0],
            device_id=(to, c), device_id_type=MESH)

    @pl.when(r == 0)
    def _():
        top[...] = jnp.zeros_like(top)
        near[1] = jnp.zeros((S, B), F32)
        recv[1] = jnp.zeros((S, cols), F32)

    @pl.when(r == R - 1)
    def _():
        near[0] = jnp.zeros((S, B), F32)
        recv[0] = jnp.zeros((S, cols), F32)

    vt[...] = jnp.zeros_like(vt)

    @pl.loop(0, LOADS)
    def _(i):
        part = pl.ds(pl.multiple_of(i * step, step), step)
        pltpu.make_async_copy(e_hbm.at[part], e_ref.at[part], e_sem.at[i]).wait()
        hi, lo = split(e_ref[part])
        hi_ref[part] = hi
        lo_ref[part] = lo

    off_copy.wait()
    lane = lax.broadcasted_iota(jnp.int32, (S, B), 1)
    sub = lax.broadcasted_iota(jnp.int32, (S, B), 0)

    everyone = pltpu.make_async_remote_copy(
        src_ref=gat.at[0:C - 1], dst_ref=gat.at[0:C - 1], send_sem=out_sem, recv_sem=gat_sem,
        device_id=(r, lax.rem(c + 1, C)), device_id_type=MESH)
    everyone.wait_recv()

    parts = [gat[q] for q in range(C)]
    blocks = [(lane >= q * piece) & (lane < (q + 1) * piece) for q in range(C)]

    def pick(tiles):
        out = tiles[0]
        for q in range(1, C):
            out = jnp.where(blocks[q], tiles[q], out)
        return out

    moved = []
    for d in range(C):
        y = pick([parts[(s + d) % C] for s in range(S)])
        moved.append(y if d == 0 else pltpu.roll(y, d * piece, 1))
    turned, heres, overs, taus = [], [], [], []
    for s in range(S):
        x = pick([moved[(q - s) % C] for q in range(C)])
        o = off_ref[s]
        turned.append(pltpu.roll(x, o, 1))
    edge[...] = gather_rows(turned, W - 1)

    @pl.when(has_down)
    def _():
        edge_copy(down).start()

    for s in range(S):
        x, o = turned[s], off_ref[s]
        here = jnp.where(lane >= o, x, 0.0)
        over = jnp.where(lane < o, x, 0.0)
        whole = here * here + jnp.where((sub < W - 1) | has_down, over * over, 0.0)
        taus.append(2.0 / (lane_sum(whole) + EPS))
        over = jnp.where(sub < W - 1, over, 0.0)
        heres.append(here)
        overs.append(over)
        fact[s] = jnp.where(sub < W - 1, taus[s], 0.0)
    tau_low = gather_rows(taus, W - 1)
    for q in range(S // 2):
        for t in range(W):
            pair = []
            for s in (2 * q, 2 * q + 1):
                x = jnp.where(sub == t, heres[s], 0.0)
                if t > 0:
                    x = x + jnp.where(sub == t - 1, overs[s], 0.0)
                pair.append(x)
            hi, lo = split(jnp.concatenate(pair, axis=0))
            at = pl.ds(t * B, B)
            vt[q * 2 * W:(q + 1) * 2 * W, at] = hi
            vt[N + q * 2 * W:N + (q + 1) * 2 * W, at] = lo
            vt[2 * N + q * 2 * W:2 * N + (q + 1) * 2 * W, at] = hi

    def pair_index(s, t):
        return s * (s - 1) // 2 + t

    for s in range(S):
        for t in range(s):
            own = lane_sum(heres[s] * heres[t] + overs[s] * overs[t])
            after = lane_sum(overs[s] * pltpu.roll(heres[t], W - 1, 0))
            before = lane_sum(heres[s] * pltpu.roll(overs[t], 1, 0))
            n = pair_index(s, t)
            coef[0, n] = own
            coef[1, n] = after
            coef[2, n] = before

    def solved(u, w):
        return solve(
            u, lambda s, t: coef[0, pair_index(s, t)], lambda s, t: coef[1, pair_index(s, t)],
            lambda s, t: coef[2, pair_index(s, t)], lambda s: fact[s], w)

    def top_part():
        @pl.when(has_up)
        def _():
            edge_copy(up).wait_recv()

        off = jnp.zeros((S, B), jnp.int32)
        for s in range(S):
            off = jnp.where(sub == s, off_ref[s], off)
        x = top[...]
        tau_top = jnp.where(has_up, 2.0 / (lane_sum(x * x) + EPS), 0.0)
        x = jnp.where(lane < off, x, 0.0)
        hi, lo = split(jnp.concatenate([jnp.zeros((S, B), F32), x], axis=0))
        vt[I:N, 0:B] = hi
        vt[N + I:2 * N, 0:B] = lo
        vt[2 * N + I:3 * N, 0:B] = hi
        first = gather_rows(heres, 0)
        into = [jnp.where(sub > s, lane_sum(x * row_of(heres[s], 0)), 0.0) for s in range(S)]
        meet = jnp.zeros((S, B), F32)
        tops = jnp.zeros((S, B), F32)
        for t in range(S):
            mark = (lane == I + S + t) & (sub > t)
            meet = jnp.where(mark, lane_sum(first * row_of(x, t)), meet)
            tops = jnp.where(mark, lane_sum(x * row_of(x, t)), tops)
        answer = []
        for s in range(S):
            y = jnp.where(sub == 0, row_of(meet, s), 0.0)
            for t in range(s):
                n = pair_index(s, t)
                y = jnp.where(lane == I + t, jnp.where(sub == W - 1, coef[0, n], jnp.where(sub == W - 2, coef[1, n], 0.0)), y)
            answer.append(y)
        p_m, c_m = solved(answer, B)
        a_low = gather_rows(p_m, W - 1)
        a_top = tops
        for s in range(S):
            a_top = a_top - into[s] * row_of(c_m[s], 0)
        msg[0] = a_top
        msg[1] = a_low

        v_top = jnp.concatenate([hi, lo], axis=0)

        for i, has, there in ((0, has_up, up), (1, has_down, down)):
            @pl.when(has)
            def _():
                msg_copy(i, there).start()
        return v_top, into, tau_top, a_top, a_low, c_m

    def top_sums(j):
        at = pl.ds(j * width, width)
        both = jnp.dot(v_top, hi_ref[0:B, at], preferred_element_type=F32)
        acc = both[S:2 * S] + both[3 * S:] + jnp.dot(v_top[:2 * S], lo_ref[0:B, at], preferred_element_type=F32)[S:]
        for s in range(S):
            acc = acc - wide(into[s], width) * jnp.broadcast_to(first_rows[j][s], (S, width))
        top_ref[:, at] = acc

        @pl.when(has_up)
        def _():
            sum_copy(0, j, up).start()

    first_rows = []
    for j in range(CHUNKS):
        at = pl.ds(j * width, width)
        both = jnp.dot(vt[0:2 * N, :], hi_ref[:, at], preferred_element_type=F32)
        u = both[:I] + both[N:N + I] + jnp.dot(vt[0:I, :], lo_ref[:, at], preferred_element_type=F32)
        p, cs = solved([u[s * W:(s + 1) * W] for s in range(S)], width)
        low_ref[:, at] = gather_rows(p, W - 1)

        @pl.when(has_down)
        def _():
            sum_copy(1, j, down).start()

        first_rows.append([x[0:1] for x in cs])
        for q in range(S // 2):
            hi, lo = split(jnp.concatenate(cs[2 * q:2 * q + 2], axis=0))
            c_ref[q * 2 * W:(q + 1) * 2 * W, at] = hi
            c_ref[N + q * 2 * W:N + (q + 1) * 2 * W, at] = lo
            c_ref[2 * N + q * 2 * W:2 * N + (q + 1) * 2 * W, at] = hi

        if j == TOP:
            v_top, into, tau_top, a_top, a_low, c_m = top_part()
            for i in range(j):
                top_sums(i)
        if j >= TOP:
            top_sums(j)

    k_t = []
    for s in range(S):
        x = jnp.where((lane == s * W + sub) & (sub < W - 1), 1.0, 0.0) - c_m[s]
        k_t.append(x + jnp.where((sub == W - 1) & (lane == I + s), 1.0, 0.0))
    k_t.append(jnp.zeros((S, B), F32))
    k_t.append(jnp.where(lane == I + S + sub, 1.0, 0.0))
    k_t = jnp.concatenate(k_t, axis=0)[:, :N]
    k_t = jnp.concatenate([k_t, k_t, k_t], axis=1)
    hi, lo = split(k_t)
    k_t = jnp.concatenate([hi, hi, lo], axis=0)
    y = lax.dot_general(vt[...], k_t, (((0,), (0,)), ((), ())), preferred_element_type=F32)
    hi, lo = split(y)
    spot = lax.broadcasted_iota(jnp.int32, y.shape, 1)
    y_ref[...] = jnp.where(spot < 2 * N, hi, lo)

    @pl.when(has_down)
    def _():
        msg_copy(0, down).wait_recv()

    @pl.when(has_up)
    def _():
        msg_copy(1, up).wait_recv()

    a_low = a_low + pltpu.roll(near[0], B - S, 1)
    a_top = a_top + pltpu.roll(near[1], S, 1)
    low_cols = [jnp.broadcast_to(a_low[:, I + t:I + t + 1], (S, B)) for t in range(S)]
    top_cols = [jnp.broadcast_to(a_top[:, I + S + t:I + S + t + 1], (S, B)) for t in range(S)]
    for j in range(CHUNKS):
        at = pl.ds(j * width, width)

        @pl.when(has_down)
        def _():
            sum_copy(0, j, down).wait_recv()

        @pl.when(has_up)
        def _():
            sum_copy(1, j, up).wait_recv()

        both = []
        for ref, i, tau, a in ((low_ref, 0, tau_low, low_cols), (top_ref, 1, tau_top, top_cols)):
            acc = ref[:, at] + recv[i, :, at]
            for t in range(S - 1):
                acc = acc - wide(a[t], width) * row_of(acc * wide(tau, width), t)
            both.append(acc * wide(tau, width))
        hi, lo = split(jnp.concatenate(both, axis=0))
        c_ref[I:N, at] = hi
        c_ref[N + I:2 * N, at] = lo
        c_ref[2 * N + I:3 * N, at] = hi

    everyone.wait_send()

    @pl.when(has_up)
    def _():
        msg_copy(0, up).wait_send()
        sums_sent(0, up).wait_send()

    @pl.when(has_down)
    def _():
        edge_copy(down).wait_send()
        msg_copy(1, down).wait_send()
        sums_sent(1, down).wait_send()


def second_kernel(parts, e_ref, y_ref, c_ref, o_hbm, buf, sem):
    width = buf.shape[1] // parts

    def store(j):
        at = pl.ds(pl.multiple_of(j * width, width), width)
        return pltpu.make_async_copy(buf.at[:, at], o_hbm.at[:, at], sem)

    @pl.loop(0, parts)
    def _(j):
        at = pl.ds(pl.multiple_of(j * width, width), width)
        buf[:, at] = e_ref[:, at] - jnp.dot(y_ref[...], c_ref[:, at], preferred_element_type=F32)
        store(j).start()

    pltpu.make_async_copy(buf, o_hbm, sem).wait()


def solution(mesh):
    R, C = mesh.shape["row"], mesh.shape["col"]

    def body(vectors_in, reflectors, offsets):
        rows, cols = vectors_in.shape
        chunks = 2 if cols % 2048 == 0 else 1
        vmem = pl.BlockSpec(memory_space=pltpu.VMEM)
        anywhere = pl.BlockSpec(memory_space=pl.ANY)
        dma = pltpu.SemaphoreType.DMA
        e, y, coeff = pl.pallas_call(
            functools.partial(first_kernel, R, C, chunks),
            out_shape=(
                pltpu.VMEM((rows, cols), F32),
                pltpu.VMEM((rows, 3 * N), BF16),
                pltpu.VMEM((3 * N, cols), BF16),
            ),
            in_specs=[anywhere] * 3,
            out_specs=(vmem, vmem, vmem),
            scratch_shapes=[
                pltpu.SMEM((S,), jnp.int32),
                pltpu.VMEM(reflectors.shape, F32),
                pltpu.VMEM((W, B), F32),
                pltpu.VMEM((C, W, B), F32),
                pltpu.VMEM((rows, cols), BF16),
                pltpu.VMEM((rows, cols), BF16),
                pltpu.VMEM((3 * N, rows), BF16),
                pltpu.VMEM((3, S * (S - 1) // 2, W, B), F32),
                pltpu.VMEM((S, W, B), F32),
                pltpu.VMEM((S, B), F32),
                pltpu.VMEM((S, B), F32),
                pltpu.VMEM((S, cols), F32),
                pltpu.VMEM((S, cols), F32),
                pltpu.VMEM((2, S, B), F32),
                pltpu.VMEM((2, S, B), F32),
                pltpu.VMEM((2, S, cols), F32),
                dma, dma, dma((LOADS,)), dma, dma, dma, dma,
                dma((2,)), dma((2,)), dma((2,)), dma((2, chunks)),
            ],
            compiler_params=pltpu.CompilerParams(
                collective_id=0, has_side_effects=True, vmem_limit_bytes=24 * MIB
            ),
            name="reflect_one",
        )(
            pltpu.with_memory_space_constraint(offsets, pltpu.HBM),
            pltpu.with_memory_space_constraint(vectors_in, pltpu.HBM),
            pltpu.with_memory_space_constraint(reflectors, pltpu.HBM),
        )
        parts = max(1, cols // 256)
        return pl.pallas_call(
            functools.partial(second_kernel, parts),
            out_shape=jax.ShapeDtypeStruct((rows, cols), F32),
            in_specs=[vmem, vmem, vmem],
            out_specs=anywhere,
            scratch_shapes=[pltpu.VMEM((rows, cols), F32), dma],
            compiler_params=pltpu.CompilerParams(vmem_limit_bytes=16 * MIB),
            name="reflect_two",
        )(*(pltpu.with_memory_space_constraint(x, pltpu.VMEM) for x in (e, y, coeff)))

    in_specs = (P("row", "col"), P(None, "row", "col"), P())
    return jax.shard_map(body, mesh=mesh, in_specs=in_specs, out_specs=P("row", "col"), check_vma=False)
```

```python
import functools

import jax
import jax.numpy as jnp
from jax import lax
from jax.experimental import pallas as pl
from jax.experimental.pallas import tpu as pltpu
from jax.sharding import PartitionSpec as P

MESH = pl.DeviceIdType.MESH
F32 = jnp.float32
BF16 = jnp.bfloat16
EPS = 1e-6
S = 8
W = 8
B = 128
I = S * W
N = I + 2 * S
LOADS = 4
EARLY = 2
MIB = 1 << 20


def split(x):
    hi = x.astype(BF16)
    return hi, (x - hi.astype(F32)).astype(BF16)


def wide(x, width):
    return jnp.concatenate([x] * (width // B), axis=1) if width > B else x


def row_of(x, i):
    return jnp.broadcast_to(x[i:i + 1], x.shape)


def gather_rows(tiles, i):
    sub = lax.broadcasted_iota(jnp.int32, tiles[0].shape, 0)
    out = jnp.zeros_like(tiles[0])
    for s, tile in enumerate(tiles):
        out = jnp.where(sub == s, row_of(tile, i), out)
    return out


def lane_sum(x):
    return jnp.broadcast_to(jnp.sum(x, axis=1, keepdims=True), x.shape)


def solve(u, own, after, before, tau, width):
    p, c, nexts, prevs = [], [], [], []
    for s in range(S):
        acc = u[s]
        for t in range(s):
            acc = acc - wide(own(s, t), width) * c[t]
            acc = acc - wide(after(s, t), width) * nexts[t]
            acc = acc - wide(before(s, t), width) * prevs[t]
        p.append(acc)
        c.append(acc * wide(tau(s), width))
        nexts.append(pltpu.roll(c[s], W - 1, 0))
        prevs.append(pltpu.roll(c[s], 1, 0))
    return p, c


def first_kernel(
    R, C, CHUNKS,
    off_hbm, e_hbm, refl_hbm,
    e_ref, y_ref, c_ref,
    off_ref, refl, mine, gat, hi_ref, lo_ref, vt, coef, fact, edge, top, low_ref, top_ref, msg, near, recv,
    off_sem, refl_sem, e_sem, out_sem, gat_sem, edge_sem, top_sem, msg_sem, near_sem, p_sem, recv_sem,
):
    r = lax.axis_index("row")
    c = lax.axis_index("col")
    up = lax.max(r - 1, 0)
    down = lax.min(r + 1, R - 1)
    has_up, has_down = r > 0, r < R - 1
    rows, cols = e_ref.shape
    step = rows // LOADS
    width = cols // CHUNKS
    TOP = CHUNKS - 1
    piece = refl.shape[2]

    barrier = pltpu.get_barrier_semaphore()
    @pl.when(has_up)
    def _():
        pl.semaphore_signal(barrier, inc=1, device_id=(up, c), device_id_type=MESH)

    @pl.when(has_down)
    def _():
        pl.semaphore_signal(barrier, inc=1, device_id=(down, c), device_id_type=MESH)

    for d in range(1, C):
        pl.semaphore_signal(barrier, inc=1, device_id=(r, lax.rem(c + d, C)), device_id_type=MESH)

    refl_copy = pltpu.make_async_copy(refl_hbm, refl, refl_sem)
    refl_copy.start()
    off_copy = pltpu.make_async_copy(off_hbm, off_ref, off_sem)
    off_copy.start()
    loads = []
    for i in range(LOADS):
        part = pl.ds(i * step, step)
        loads.append(pltpu.make_async_copy(e_hbm.at[part], e_ref.at[part], e_sem.at[i]))
    for load in loads[:EARLY]:
        load.start()

    refl_copy.wait()
    tile = jnp.concatenate([refl[s] for s in range(S)], axis=1)
    mine[...] = tile
    pl.semaphore_wait(barrier, C - 1 + lax.min(r, 1) + lax.min(R - 1 - r, 1))

    sends = []
    for d in sorted(range(1, C), key=lambda d: abs(d - C // 2)):
        sends.append(pltpu.make_async_remote_copy(
            src_ref=mine, dst_ref=gat.at[c], send_sem=out_sem, recv_sem=gat_sem,
            device_id=(r, lax.rem(c + d, C)), device_id_type=MESH))
    for copy in sends:
        copy.start()
    for load in loads[EARLY:]:
        load.start()
    gat[c] = tile

    def edge_copy(to):
        return pltpu.make_async_remote_copy(
            src_ref=edge, dst_ref=top, send_sem=edge_sem, recv_sem=top_sem,
            device_id=(to, c), device_id_type=MESH)

    def msg_copy(i, to):
        return pltpu.make_async_remote_copy(
            src_ref=msg.at[i], dst_ref=near.at[i], send_sem=msg_sem.at[i], recv_sem=near_sem.at[i],
            device_id=(to, c), device_id_type=MESH)

    def sum_copy(i, j, to):
        at = pl.ds(j * width, width)
        return pltpu.make_async_remote_copy(
            src_ref=(top_ref, low_ref)[i].at[:, at], dst_ref=recv.at[i, :, at],
            send_sem=p_sem.at[i], recv_sem=recv_sem.at[i, j],
            device_id=(to, c), device_id_type=MESH)

    def sums_sent(i, to):
        return pltpu.make_async_remote_copy(
            src_ref=(top_ref, low_ref)[i], dst_ref=recv.at[i], send_sem=p_sem.at[i], recv_sem=recv_sem.at[i, 0],
            device_id=(to, c), device_id_type=MESH)

    @pl.when(r == 0)
    def _():
        top[...] = jnp.zeros_like(top)
        near[1] = jnp.zeros((S, B), F32)
        recv[1] = jnp.zeros((S, cols), F32)

    @pl.when(r == R - 1)
    def _():
        near[0] = jnp.zeros((S, B), F32)
        recv[0] = jnp.zeros((S, cols), F32)

    vt[...] = jnp.zeros_like(vt)

    @pl.loop(0, LOADS)
    def _(i):
        part = pl.ds(pl.multiple_of(i * step, step), step)
        pltpu.make_async_copy(e_hbm.at[part], e_ref.at[part], e_sem.at[i]).wait()
        hi, lo = split(e_ref[part])
        hi_ref[part] = hi
        lo_ref[part] = lo

    off_copy.wait()
    lane = lax.broadcasted_iota(jnp.int32, (S, B), 1)
    sub = lax.broadcasted_iota(jnp.int32, (S, B), 0)

    everyone = pltpu.make_async_remote_copy(
        src_ref=gat.at[0:C - 1], dst_ref=gat.at[0:C - 1], send_sem=out_sem, recv_sem=gat_sem,
        device_id=(r, lax.rem(c + 1, C)), device_id_type=MESH)
    everyone.wait_recv()

    parts = [gat[q] for q in range(C)]
    blocks = [(lane >= q * piece) & (lane < (q + 1) * piece) for q in range(C)]

    def pick(tiles):
        out = tiles[0]
        for q in range(1, C):
            out = jnp.where(blocks[q], tiles[q], out)
        return out

    moved = []
    for d in range(C):
        y = pick([parts[(s + d) % C] for s in range(S)])
        moved.append(y if d == 0 else pltpu.roll(y, d * piece, 1))
    turned, heres, overs, taus = [], [], [], []
    for s in range(S):
        x = pick([moved[(q - s) % C] for q in range(C)])
        o = off_ref[s]
        turned.append(pltpu.roll(x, o, 1))
    edge[...] = gather_rows(turned, W - 1)

    @pl.when(has_down)
    def _():
        edge_copy(down).start()

    for s in range(S):
        x, o = turned[s], off_ref[s]
        here = jnp.where(lane >= o, x, 0.0)
        over = jnp.where(lane < o, x, 0.0)
        whole = here * here + jnp.where((sub < W - 1) | has_down, over * over, 0.0)
        taus.append(2.0 / (lane_sum(whole) + EPS))
        over = jnp.where(sub < W - 1, over, 0.0)
        heres.append(here)
        overs.append(over)
        fact[s] = jnp.where(sub < W - 1, taus[s], 0.0)
    tau_low = gather_rows(taus, W - 1)
    for q in range(S // 2):
        for t in range(W):
            pair = []
            for s in (2 * q, 2 * q + 1):
                x = jnp.where(sub == t, heres[s], 0.0)
                if t > 0:
                    x = x + jnp.where(sub == t - 1, overs[s], 0.0)
                pair.append(x)
            hi, lo = split(jnp.concatenate(pair, axis=0))
            at = pl.ds(t * B, B)
            vt[q * 2 * W:(q + 1) * 2 * W, at] = hi
            vt[N + q * 2 * W:N + (q + 1) * 2 * W, at] = lo
            vt[2 * N + q * 2 * W:2 * N + (q + 1) * 2 * W, at] = hi

    def pair_index(s, t):
        return s * (s - 1) // 2 + t

    for s in range(S):
        for t in range(s):
            own = lane_sum(heres[s] * heres[t] + overs[s] * overs[t])
            after = lane_sum(overs[s] * pltpu.roll(heres[t], W - 1, 0))
            before = lane_sum(heres[s] * pltpu.roll(overs[t], 1, 0))
            n = pair_index(s, t)
            coef[0, n] = own
            coef[1, n] = after
            coef[2, n] = before

    def solved(u, w):
        return solve(
            u, lambda s, t: coef[0, pair_index(s, t)], lambda s, t: coef[1, pair_index(s, t)],
            lambda s, t: coef[2, pair_index(s, t)], lambda s: fact[s], w)

    off = jnp.zeros((S, B), jnp.int32)
    for s in range(S):
        off = jnp.where(sub == s, off_ref[s], off)
    firsts = [row_of(heres[s], 0) for s in range(S)]

    def top_part():
        @pl.when(has_up)
        def _():
            edge_copy(up).wait_recv()

        x = top[...]
        tau_top = jnp.where(has_up, 2.0 / (lane_sum(x * x) + EPS), 0.0)
        x = jnp.where(lane < off, x, 0.0)
        hi, lo = split(jnp.concatenate([jnp.zeros((S, B), F32), x], axis=0))
        vt[I:N, 0:B] = hi
        vt[N + I:2 * N, 0:B] = lo
        vt[2 * N + I:3 * N, 0:B] = hi
        first = gather_rows(heres, 0)
        into = [jnp.where(sub > s, lane_sum(x * firsts[s]), 0.0) for s in range(S)]
        meet = jnp.zeros((S, B), F32)
        tops = jnp.zeros((S, B), F32)
        for t in range(S):
            mark = (lane == I + S + t) & (sub > t)
            meet = jnp.where(mark, lane_sum(first * row_of(x, t)), meet)
            tops = jnp.where(mark, lane_sum(x * row_of(x, t)), tops)
        answer = []
        for s in range(S):
            y = jnp.where(sub == 0, row_of(meet, s), 0.0)
            for t in range(s):
                n = pair_index(s, t)
                y = jnp.where(lane == I + t, jnp.where(sub == W - 1, coef[0, n], jnp.where(sub == W - 2, coef[1, n], 0.0)), y)
            answer.append(y)
        p_m, c_m = solved(answer, B)
        a_low = gather_rows(p_m, W - 1)
        a_top = tops
        for s in range(S):
            a_top = a_top - into[s] * row_of(c_m[s], 0)
        msg[0] = a_top
        msg[1] = a_low

        v_top = jnp.concatenate([hi, lo], axis=0)

        for i, has, there in ((0, has_up, up), (1, has_down, down)):
            @pl.when(has)
            def _():
                msg_copy(i, there).start()
        return v_top, into, tau_top, a_top, a_low, c_m

    def top_sums(j):
        at = pl.ds(j * width, width)
        both = jnp.dot(v_top, hi_ref[0:B, at], preferred_element_type=F32)
        acc = both[S:2 * S] + both[3 * S:] + jnp.dot(v_top[:2 * S], lo_ref[0:B, at], preferred_element_type=F32)[S:]
        for s in range(S):
            acc = acc - wide(into[s], width) * jnp.broadcast_to(first_rows[j][s], (S, width))
        top_ref[:, at] = acc

        @pl.when(has_up)
        def _():
            sum_copy(0, j, up).start()

    first_rows = []
    for j in range(CHUNKS):
        at = pl.ds(j * width, width)
        both = jnp.dot(vt[0:2 * N, :], hi_ref[:, at], preferred_element_type=F32)
        u = both[:I] + both[N:N + I] + jnp.dot(vt[0:I, :], lo_ref[:, at], preferred_element_type=F32)
        p, cs = solved([u[s * W:(s + 1) * W] for s in range(S)], width)
        low_ref[:, at] = gather_rows(p, W - 1)

        @pl.when(has_down)
        def _():
            sum_copy(1, j, down).start()

        first_rows.append([x[0:1] for x in cs])
        for q in range(S // 2):
            hi, lo = split(jnp.concatenate(cs[2 * q:2 * q + 2], axis=0))
            c_ref[q * 2 * W:(q + 1) * 2 * W, at] = hi
            c_ref[N + q * 2 * W:N + (q + 1) * 2 * W, at] = lo
            c_ref[2 * N + q * 2 * W:2 * N + (q + 1) * 2 * W, at] = hi

        if j == TOP:
            v_top, into, tau_top, a_top, a_low, c_m = top_part()
            for i in range(j):
                top_sums(i)
        if j >= TOP:
            top_sums(j)

    k_t = []
    for s in range(S):
        x = jnp.where((lane == s * W + sub) & (sub < W - 1), 1.0, 0.0) - c_m[s]
        k_t.append(x + jnp.where((sub == W - 1) & (lane == I + s), 1.0, 0.0))
    k_t.append(jnp.zeros((S, B), F32))
    k_t.append(jnp.where(lane == I + S + sub, 1.0, 0.0))
    k_t = jnp.concatenate(k_t, axis=0)[:, :N]
    k_t = jnp.concatenate([k_t, k_t, k_t], axis=1)
    hi, lo = split(k_t)
    k_t = jnp.concatenate([hi, hi, lo], axis=0)
    y = lax.dot_general(vt[...], k_t, (((0,), (0,)), ((), ())), preferred_element_type=F32)
    hi, lo = split(y)
    spot = lax.broadcasted_iota(jnp.int32, y.shape, 1)
    y_ref[...] = jnp.where(spot < 2 * N, hi, lo)

    @pl.when(has_down)
    def _():
        msg_copy(0, down).wait_recv()

    @pl.when(has_up)
    def _():
        msg_copy(1, up).wait_recv()

    a_low = a_low + pltpu.roll(near[0], B - S, 1)
    a_top = a_top + pltpu.roll(near[1], S, 1)
    low_cols = [jnp.broadcast_to(a_low[:, I + t:I + t + 1], (S, B)) for t in range(S)]
    top_cols = [jnp.broadcast_to(a_top[:, I + S + t:I + S + t + 1], (S, B)) for t in range(S)]
    for j in range(CHUNKS):
        at = pl.ds(j * width, width)

        @pl.when(has_down)
        def _():
            sum_copy(0, j, down).wait_recv()

        @pl.when(has_up)
        def _():
            sum_copy(1, j, up).wait_recv()

        both = []
        for ref, i, tau, a in ((low_ref, 0, tau_low, low_cols), (top_ref, 1, tau_top, top_cols)):
            acc = ref[:, at] + recv[i, :, at]
            for t in range(S - 1):
                acc = acc - wide(a[t], width) * row_of(acc * wide(tau, width), t)
            both.append(acc * wide(tau, width))
        hi, lo = split(jnp.concatenate(both, axis=0))
        c_ref[I:N, at] = hi
        c_ref[N + I:2 * N, at] = lo
        c_ref[2 * N + I:3 * N, at] = hi

    everyone.wait_send()

    @pl.when(has_up)
    def _():
        msg_copy(0, up).wait_send()
        sums_sent(0, up).wait_send()

    @pl.when(has_down)
    def _():
        edge_copy(down).wait_send()
        msg_copy(1, down).wait_send()
        sums_sent(1, down).wait_send()


def second_kernel(parts, e_ref, y_ref, c_ref, o_hbm, buf, sem):
    width = buf.shape[1] // parts

    def store(j):
        at = pl.ds(pl.multiple_of(j * width, width), width)
        return pltpu.make_async_copy(buf.at[:, at], o_hbm.at[:, at], sem)

    @pl.loop(0, parts)
    def _(j):
        at = pl.ds(pl.multiple_of(j * width, width), width)
        buf[:, at] = e_ref[:, at] - jnp.dot(y_ref[...], c_ref[:, at], preferred_element_type=F32)
        store(j).start()

    pltpu.make_async_copy(buf, o_hbm, sem).wait()


def solution(mesh):
    R, C = mesh.shape["row"], mesh.shape["col"]

    def body(vectors_in, reflectors, offsets):
        rows, cols = vectors_in.shape
        chunks = 2 if cols % 2048 == 0 else 1
        vmem = pl.BlockSpec(memory_space=pltpu.VMEM)
        anywhere = pl.BlockSpec(memory_space=pl.ANY)
        dma = pltpu.SemaphoreType.DMA
        e, y, coeff = pl.pallas_call(
            functools.partial(first_kernel, R, C, chunks),
            out_shape=(
                pltpu.VMEM((rows, cols), F32),
                pltpu.VMEM((rows, 3 * N), BF16),
                pltpu.VMEM((3 * N, cols), BF16),
            ),
            in_specs=[anywhere] * 3,
            out_specs=(vmem, vmem, vmem),
            scratch_shapes=[
                pltpu.SMEM((S,), jnp.int32),
                pltpu.VMEM(reflectors.shape, F32),
                pltpu.VMEM((W, B), F32),
                pltpu.VMEM((C, W, B), F32),
                pltpu.VMEM((rows, cols), BF16),
                pltpu.VMEM((rows, cols), BF16),
                pltpu.VMEM((3 * N, rows), BF16),
                pltpu.VMEM((3, S * (S - 1) // 2, W, B), F32),
                pltpu.VMEM((S, W, B), F32),
                pltpu.VMEM((S, B), F32),
                pltpu.VMEM((S, B), F32),
                pltpu.VMEM((S, cols), F32),
                pltpu.VMEM((S, cols), F32),
                pltpu.VMEM((2, S, B), F32),
                pltpu.VMEM((2, S, B), F32),
                pltpu.VMEM((2, S, cols), F32),
                dma, dma, dma((LOADS,)), dma, dma, dma, dma,
                dma((2,)), dma((2,)), dma((2,)), dma((2, chunks)),
            ],
            compiler_params=pltpu.CompilerParams(
                collective_id=0, has_side_effects=True, vmem_limit_bytes=24 * MIB
            ),
            name="reflect_one",
        )(
            pltpu.with_memory_space_constraint(offsets, pltpu.HBM),
            pltpu.with_memory_space_constraint(vectors_in, pltpu.HBM),
            pltpu.with_memory_space_constraint(reflectors, pltpu.HBM),
        )
        parts = max(1, cols // 256)
        return pl.pallas_call(
            functools.partial(second_kernel, parts),
            out_shape=jax.ShapeDtypeStruct((rows, cols), F32),
            in_specs=[vmem, vmem, vmem],
            out_specs=anywhere,
            scratch_shapes=[pltpu.VMEM((rows, cols), F32), dma],
            compiler_params=pltpu.CompilerParams(vmem_limit_bytes=16 * MIB),
            name="reflect_two",
        )(*(pltpu.with_memory_space_constraint(x, pltpu.VMEM) for x in (e, y, coeff)))

    in_specs = (P("row", "col"), P(None, "row", "col"), P())
    return jax.shard_map(body, mesh=mesh, in_specs=in_specs, out_specs=P("row", "col"), check_vma=False)
```
